512 devices in a mesh: row: 16 (over y, core), col: 32 (over z, x).
Axes of the slice: x: 4, y: 8, z: 8, core: 2. Of those that a mesh axis runs over, the one named last changes fastest.
Arguments:
- acts: bfloat16 [192, 2, 28672], P('col', None, 'row'), may hold values from -6 to 6
- grads: bfloat16 [192, 2, 8192], P('row', None, 'col'), may hold values from -0.3984375 to 0.3984375
- basis_in: bfloat16 [28672, 28672], P('row', 'col'), may hold values from -0.03125 to 0.03125
- basis_out: bfloat16 [8192, 8192], P('col', 'row'), may hold values from -0.0625 to 0.0625
- eigen: bfloat16 [28672, 8192], P('col', 'row'), may hold values from 0.5 to 8
- sketch: bfloat16 [72, 8192], P(None, 'col'), may hold values from -0.0625 to 0.0625
Outputs:
- range_basis: float32 [2, 72, 28672], P(None, None, 'row')
- projected: float32 [2, 72, 8192], P(None, None, 'col')
The draws below stay inside these ranges and needn't reach their ends.
All inputs are finite; a program needn't handle non-finite values.
Results may differ from the reference program's by a relative error of at most 0.018.
Values may be sent and summed in bfloat16 or wider, within the bound.
No kernel may reach another device: no remote copies, remote signals or barrier semaphores. Data moves between devices by JAX's collectives and lax.ppermute only.
A program may use at most 64 MiB of HBM per device.

```python
import math
import jax
import jax.numpy as jnp
from jax import lax

IN = 28672
OUT = 8192
SK = 72
NQ = 2
TOK = 192


def steps_of(own_key, shape, shards, low, largest):
    loudness = 1.0
    for position, parts in shards:
        steps = jax.random.uniform(jax.random.fold_in(jax.random.fold_in(own_key, 6), position), (parts,), jnp.float32, low / len(shards), largest / len(shards))
        loudness = loudness * jnp.repeat(jnp.exp(steps), shape[position] // parts).reshape((-1,) + (1,) * (len(shape) - 1 - position))
    return loudness


def bell_draw(rng, shape, spread, bound, shards=(), dtype=jnp.bfloat16):
    level = steps_of(rng, shape, shards, -0.22, 0.18) if shards else 1.0
    values = jax.random.normal(rng, shape, jnp.float32) * spread * level
    return jnp.minimum(jnp.maximum(values, -bound), bound).astype(dtype)


def setup_inputs(seed: int = 0) -> dict:
    splits = jax.random.split(jax.random.key(seed), 7)
    return {
        "acts": bell_draw(splits[0], (TOK, NQ, IN), 1.0, 6.0, ((0, 32), (2, 16))),
        "grads": bell_draw(splits[1], (TOK, NQ, OUT), 0.0625, 0.3984375, ((0, 16), (2, 32))),
        "basis_in": bell_draw(splits[2], (IN, IN), IN ** -0.5, 0.03125, ((0, 16), (1, 32))),
        "basis_out": bell_draw(splits[3], (OUT, OUT), OUT ** -0.5, 0.0625, ((0, 32), (1, 16))),
        "eigen": jnp.clip(jnp.exp(math.log(8.0) - 2.7725887 * jax.random.uniform(splits[4], (IN, OUT), jnp.float32) ** steps_of(splits[4], (IN, OUT), ((0, 32), (1, 16)), -0.2, 0.2)), 0.5, 8.0).astype(jnp.bfloat16),
        "sketch": bell_draw(splits[5], (SK, OUT), OUT ** -0.5, 0.0625, ((1, 32),)),
    }


def reference(acts, grads, basis_in, basis_out, eigen, sketch):
    act_rot = jnp.dot(acts.reshape(TOK * NQ, IN).astype(jnp.float32), basis_in.astype(jnp.float32), preferred_element_type=jnp.float32).astype(jnp.bfloat16).reshape(TOK, NQ, IN)
    grad_rot = jnp.dot(grads.reshape(TOK * NQ, OUT).astype(jnp.float32), basis_out.astype(jnp.float32), preferred_element_type=jnp.float32).astype(jnp.bfloat16).reshape(TOK, NQ, OUT)
    sketch_rot = jnp.dot(sketch.astype(jnp.float32), basis_out.astype(jnp.float32), preferred_element_type=jnp.float32).astype(jnp.bfloat16)
    eigen_wide = eigen.astype(jnp.float32)
    bases = []
    projections = []
    for query in range(NQ):
        core_sum = jnp.dot(act_rot[:, query, :].T.astype(jnp.float32), grad_rot[:, query, :].astype(jnp.float32), preferred_element_type=jnp.float32)
        scaled = (core_sum / eigen_wide).astype(jnp.bfloat16)
        reduced = jnp.dot(sketch_rot.astype(jnp.float32), scaled.T.astype(jnp.float32), preferred_element_type=jnp.float32).astype(jnp.bfloat16)
        range_rows = jnp.dot(reduced.astype(jnp.float32), basis_in.T.astype(jnp.float32), preferred_element_type=jnp.float32)
        gram = jnp.dot(range_rows, range_rows.T, precision=lax.Precision.HIGHEST)
        factor = jnp.linalg.cholesky(gram)
        basis_rows = lax.linalg.triangular_solve(factor, range_rows, left_side=True, lower=True)
        mapped = jnp.dot(basis_rows.astype(jnp.bfloat16).astype(jnp.float32), basis_in.astype(jnp.float32), preferred_element_type=jnp.float32).astype(jnp.bfloat16)
        core = jnp.dot(mapped.astype(jnp.float32), scaled.astype(jnp.float32), preferred_element_type=jnp.float32).astype(jnp.bfloat16)
        projection = jnp.dot(core.astype(jnp.float32), basis_out.T.astype(jnp.float32), preferred_element_type=jnp.float32)
        bases.append(basis_rows)
        projections.append(projection)
    return (jnp.stack(bases), jnp.stack(projections))
```

```python
import functools

import jax
import jax.numpy as jnp
from jax import lax
from jax.experimental import pallas as pl
from jax.experimental.pallas import tpu as pltpu
from jax.sharding import Mesh
from jax.sharding import PartitionSpec as P

COL = ("z", "x")
ROW = ("y", "core")
BF = jnp.bfloat16
F32 = jnp.float32
MIB = 1024 * 1024


def call(body, out, *args, limit=32):
    many = isinstance(out, list)
    shapes = [jax.ShapeDtypeStruct(s, d) for s, d in (out if many else [out])]
    got = pl.pallas_call(
        body,
        out_shape=shapes,
        in_specs=[
            pl.BlockSpec(memory_space=pltpu.SMEM if a.size == 1 else pltpu.VMEM) for a in args
        ],
        out_specs=[pl.BlockSpec(memory_space=pltpu.VMEM)] * len(shapes),
        compiler_params=pltpu.CompilerParams(vmem_limit_bytes=limit * MIB),
    )(*args)
    return got if many else got[0]


def swap(x, axes):
    return lax.all_to_all(x, axes, 0, 0, tiled=True)


def dot(a, b, ca=1, cb=0, **kw):
    return lax.dot_general(a, b, (((ca,), (cb,)), ((), ())), preferred_element_type=F32, **kw)


def to_tiles(y, out_ref, slots):
    lanes = y.shape[1] // 128
    count = (y.shape[0] // 16) * lanes
    y = y.astype(BF)
    for t in range(out_ref.shape[0] * slots):
        if t < count:
            r, g = divmod(t, lanes)
            tile = y[r * 16 : r * 16 + 16, g * 128 : g * 128 + 128]
        else:
            tile = jnp.zeros((16, 128), BF)
        out_ref[t // slots, t % slots] = tile


def from_tiles(ref, slots, rows, lanes):
    lines = []
    for r in range(rows):
        at = [divmod(r * lanes + g, slots) for g in range(lanes)]
        lines.append(jnp.concatenate([ref[p, s] for p, s in at], axis=1))
    return jnp.concatenate(lines, axis=0)


def sum_body(x_ref, out_ref):
    total = jnp.sum(x_ref[...].astype(F32), axis=0).astype(BF)
    out_ref[...] = jnp.broadcast_to(total[None], out_ref.shape)


def sum_over(pieces, axes):
    own = swap(pieces, axes)
    return swap(call(sum_body, (own.shape, BF), own), axes)


def pack_body(x_ref, out_ref):
    x = x_ref[...].astype(F32)
    half = x.shape[1] // 2
    first, rest = x[:8], x[8:]
    low, high = rest[:, :half], rest[:, half:]
    rest = jnp.concatenate([low, high], axis=0)
    wide = out_ref.shape[2]
    left = x.shape[1] - wide
    spare = jnp.zeros((8, 2 * wide - x.shape[1] - half), F32)
    bottom = jnp.concatenate([first[:, wide:], rest, spare], axis=1)
    assert left + half + spare.shape[1] == wide
    packed = jnp.concatenate([first[:, :wide], bottom], axis=0).astype(BF)
    out_ref[...] = jnp.broadcast_to(packed[None], out_ref.shape)


def act_body(x_ref, w_ref, out_ref):
    v = x_ref[...].astype(F32)
    wide = v.shape[2]
    full = w_ref.shape[0]
    half = full // 2
    top, bottom = v[:, :8], v[:, 8:]
    left = full - wide
    first = jnp.concatenate([top, bottom[:, :, :left]], axis=2)
    rest = bottom[:, :, left : left + half].reshape(v.shape[0] // 2, 2, 8, half)
    even, odd = rest[:, 0], rest[:, 1]
    head = lax.broadcasted_iota(jnp.int32, even.shape, 1) < 4
    low = jnp.where(head, even, pltpu.roll(odd, 4, 1))
    high = jnp.where(head, pltpu.roll(even, 4, 1), odd)
    last = jnp.concatenate([low, high], axis=2)
    pairs = first.reshape(v.shape[0] // 2, 16, full)
    x = jnp.concatenate([pairs, last], axis=1).reshape(v.shape[0] * 12, full).astype(BF)
    out_ref[...] = dot(x, w_ref[...]).astype(BF)


def grad_body(g_ref, s_ref, w_ref, out_ref):
    w = w_ref[...]
    n = g_ref.shape[0]
    out_ref[:n] = dot(g_ref[...], w).astype(BF)
    s = dot(s_ref[...], w)
    spare = jnp.zeros((out_ref.shape[0] - n - s.shape[0], s.shape[1]), F32)
    out_ref[n:] = jnp.concatenate([s, spare], axis=0).astype(BF)


def scaled_body(a_ref, g_ref, e_ref, scaled_ref, out_ref):
    n = a_ref.shape[0]
    a = a_ref[...].T
    g = g_ref[:n]
    sk = g_ref[n : n + 80]
    odd = lax.broadcasted_iota(jnp.int32, g.shape, 0) % 2
    e = e_ref[...].astype(F32)
    parts = []
    for q in range(2):
        mine = jnp.where(odd == q, g.astype(F32), 0.0).astype(BF)
        s = (dot(a, mine) / e).astype(BF)
        scaled_ref[q] = s
        parts.append(dot(sk, s, 1, 1)[:72])
    to_tiles(jnp.concatenate(parts, axis=0), out_ref, out_ref.shape[1])


def range_body(r_ref, w_ref, out_ref):
    r = from_tiles(r_ref, 4, 9, 7)
    to_tiles(dot(r, w_ref[...], 1, 1), out_ref, 4)


def mapped_slot(t):
    return divmod(t, 6) if t < 42 else (7 + (t - 42) // 3, (t - 42) % 3)


def split3(x):
    hi = x.astype(BF)
    left = x - hi.astype(F32)
    mid = left.astype(BF)
    return hi, mid, (left - mid.astype(F32)).astype(BF)


def mapped_body(r_ref, w_ref, out_ref):
    r = from_tiles(r_ref, 4, 9, 14)
    y = dot(r, w_ref[...]).astype(BF)
    for t in range(69):
        p, s = mapped_slot(t)
        a, g = divmod(t, 7)
        tile = y[a * 16 : a * 16 + 16, g * 128 : g * 128 + 128] if t < 63 else jnp.zeros((16, 128), BF)
        out_ref[p, s] = tile
    wide = r.astype(F32)
    grams = []
    for q in range(2):
        rq = wide[q * 72 : q * 72 + 72].astype(BF)
        g = dot(rq, rq, 1, 1)
        grams.append(jnp.concatenate([g, jnp.zeros((72, 56), F32)], axis=1))
    gram = jnp.concatenate(grams, axis=0)
    for i, part in enumerate(split3(gram)):
        for a in range(9):
            out_ref[7 + a, 3 + i] = part[a * 16 : a * 16 + 16]


def gram_sum_body(flag_ref, x_ref, out_ref):
    total = jnp.sum(x_ref[...].astype(F32), axis=0)
    whole = total[3] + total[4] + total[5]
    plain = flag_ref[0, 0] < 7
    parts = split3(whole)
    for i in range(6):
        tile = total[i].astype(BF)
        if i >= 3:
            tile = jnp.where(plain, total[i], parts[i - 3].astype(F32)).astype(BF)
        out_ref[:, i] = jnp.broadcast_to(tile[None], (out_ref.shape[0], 16, 128))


def core_body(m_ref, s_ref, out_ref):
    tiles = [m_ref[mapped_slot(t)] for t in range(63)]
    m = jnp.concatenate(
        [jnp.concatenate(tiles[r * 7 : r * 7 + 7], axis=1) for r in range(9)], axis=0
    ).astype(F32)
    parts = [dot(m[q * 72 : q * 72 + 72].astype(BF), s_ref[q]) for q in range(2)]
    to_tiles(jnp.concatenate(parts, axis=0), out_ref, 2)


def inverse_body(m_ref, out_ref):
    gram = jnp.concatenate(
        [sum(m_ref[7 + a, 3 + i].astype(F32) for i in range(3)) for a in range(9)], axis=0
    )
    rows = lax.broadcasted_iota(jnp.int32, (72, 128), 0)
    lanes = lax.broadcasted_iota(jnp.int32, (72, 128), 1)
    below = lax.broadcasted_iota(jnp.int32, (72, 1), 0)
    eye = jnp.where(rows == lanes, 1.0, 0.0)
    left = [gram[q * 72 : q * 72 + 72] for q in range(2)]
    right = [eye, eye]
    for k in range(72):
        for q in range(2):
            pivot = left[q][k : k + 1]
            f = left[q][:, k : k + 1] / pivot[:, k : k + 1]
            f = jnp.where(below > k, f, 0.0)
            line = right[q][k : k + 1]
            left[q] = left[q] - f * pivot
            right[q] = right[q] - f * line
    for q in range(2):
        d = jnp.sum(jnp.where(rows == lanes, left[q], 0.0), axis=1, keepdims=True)
        out_ref[q] = right[q] / jnp.sqrt(d)


def basis_body(w_ref, r_ref, out_ref):
    r = from_tiles(r_ref, 4, 9, 14).astype(F32)
    for q in range(2):
        w = w_ref[q][:, :72]
        out_ref[q] = dot(w, r[q * 72 : q * 72 + 72], precision=lax.Precision.HIGHEST)


def project_body(c_ref, w_ref, out_ref):
    c = from_tiles(c_ref, 2, 9, 4)
    to_tiles(dot(c, w_ref[...], 1, 1), out_ref, 2)


def final_body(w_ref, p_ref, out_ref):
    p = from_tiles(p_ref, 2, 9, 2).astype(F32)
    for q in range(2):
        w = w_ref[q][:, :72]
        out_ref[q] = dot(w, p[q * 72 : q * 72 + 72], precision=lax.Precision.HIGHEST)


def on_device(acts, grads, basis_in, basis_out, eigen, sketch):
    g = grads.reshape(24, 256)
    g = jnp.concatenate([g[0:8], g[12:20], g[8:12], g[20:24]], axis=0)
    all_grads = swap(jnp.broadcast_to(g[None], (16, 24, 256)), ROW).reshape(384, 256)
    packed = call(pack_body, ((32, 16, 1408), BF), acts.reshape(12, 1792))
    all_acts = swap(packed, COL)
    g_part = call(grad_body, ((512, 512), BF), all_grads, sketch, basis_out)
    g_rot = sum_over(g_part.reshape(32, 16, 512), COL).reshape(512, 512)
    a_part = call(act_body, ((384, 896), BF), all_acts, basis_in)
    a_rot = sum_over(a_part.reshape(16, 24, 896), ROW).reshape(384, 896)
    scaled, red = call(
        scaled_body, [((2, 896, 512), BF), ((16, 4, 16, 128), BF)], a_rot, g_rot, eigen
    )
    reduced = sum_over(red, ROW)
    span = call(range_body, ((32, 4, 16, 128), BF), reduced, basis_in)
    span = sum_over(span, COL)
    mapped = swap(call(mapped_body, ((16, 6, 16, 128), BF), span, basis_in), ROW)
    flag = jnp.full((1, 1), lax.axis_index(ROW), jnp.int32)
    mapped = swap(call(gram_sum_body, ((16, 6, 16, 128), BF), flag, mapped), ROW)
    core = sum_over(call(core_body, ((32, 2, 16, 128), BF), mapped, scaled), COL)
    inverse = call(inverse_body, ((2, 72, 128), F32), mapped)
    basis = call(basis_body, ((2, 72, 1792), F32), inverse, span)
    proj = sum_over(call(project_body, ((16, 2, 16, 128), BF), core, basis_out), ROW)
    return basis, call(final_body, ((2, 72, 256), F32), inverse, proj)


def solution(mesh):
    split = Mesh(mesh.devices.reshape(8, 2, 8, 4), ("y", "core", "z", "x"))
    return jax.shard_map(
        on_device,
        mesh=split,
        in_specs=(
            P(COL, None, ROW),
            P(ROW, None, COL),
            P(ROW, COL),
            P(COL, ROW),
            P(COL, ROW),
            P(None, COL),
        ),
        out_specs=(P(None, None, ROW), P(None, None, COL)),
        check_vma=False,
    )
```

```python
import functools

import jax
import jax.numpy as jnp
from jax import lax
from jax.experimental import pallas as pl
from jax.experimental.pallas import tpu as pltpu
from jax.sharding import Mesh
from jax.sharding import PartitionSpec as P

COL = ("z", "x")
ROW = ("y", "core")
BF = jnp.bfloat16
F32 = jnp.float32
MIB = 1024 * 1024


def call(body, out, *args, limit=32):
    many = isinstance(out, list)
    shapes = [jax.ShapeDtypeStruct(s, d) for s, d in (out if many else [out])]
    got = pl.pallas_call(
        body,
        out_shape=shapes,
        in_specs=[pl.BlockSpec(memory_space=pltpu.VMEM)] * len(args),
        out_specs=[pl.BlockSpec(memory_space=pltpu.VMEM)] * len(shapes),
        compiler_params=pltpu.CompilerParams(vmem_limit_bytes=limit * MIB),
    )(*args)
    return got if many else got[0]


def swap(x, axes):
    return lax.all_to_all(x, axes, 0, 0, tiled=True)


def dot(a, b, ca=1, cb=0, **kw):
    return lax.dot_general(a, b, (((ca,), (cb,)), ((), ())), preferred_element_type=F32, **kw)


def to_tiles(y, out_ref, slots):
    lanes = y.shape[1] // 128
    count = (y.shape[0] // 16) * lanes
    y = y.astype(BF)
    for t in range(out_ref.shape[0] * slots):
        if t < count:
            r, g = divmod(t, lanes)
            tile = y[r * 16 : r * 16 + 16, g * 128 : g * 128 + 128]
        else:
            tile = jnp.zeros((16, 128), BF)
        out_ref[t // slots, t % slots] = tile


def from_tiles(ref, slots, rows, lanes):
    lines = []
    for r in range(rows):
        at = [divmod(r * lanes + g, slots) for g in range(lanes)]
        lines.append(jnp.concatenate([ref[p, s] for p, s in at], axis=1))
    return jnp.concatenate(lines, axis=0)


def sum_body(x_ref, out_ref):
    total = jnp.sum(x_ref[...].astype(F32), axis=0).astype(BF)
    out_ref[...] = jnp.broadcast_to(total[None], out_ref.shape)


def sum_one_body(x_ref, out_ref):
    out_ref[...] = jnp.sum(x_ref[...].astype(F32), axis=0).astype(BF)


def summed(pieces, axes):
    own = swap(pieces, axes)
    return call(sum_one_body, (own.shape[1:], BF), own)


def sum_over(pieces, axes):
    own = swap(pieces, axes)
    return swap(call(sum_body, (own.shape, BF), own), axes)


def join_body(own_ref, x_ref, out_ref):
    g = jnp.sum(own_ref[...].astype(F32), axis=0)
    x = x_ref[...].astype(F32)
    half = x.shape[1] // 2
    wide = out_ref.shape[2] - g.shape[1]
    first, rest = x[:8], x[8:]
    rest = jnp.concatenate([rest[:, :half], rest[:, half:]], axis=0)
    spare = jnp.zeros((8, 2 * wide - x.shape[1] - half), F32)
    bottom = jnp.concatenate([first[:, wide:], rest, spare], axis=1)
    packed = jnp.concatenate([first[:, :wide], bottom], axis=0)
    joined = jnp.concatenate([packed, g], axis=1).astype(BF)
    out_ref[...] = jnp.broadcast_to(joined[None], out_ref.shape)


def act_body(x_ref, w_ref, out_ref, g_ref):
    peers = [x_ref[c % 4, c // 4] for c in range(32)]
    full = w_ref.shape[0]
    half = full // 2
    wide = x_ref.shape[3] - g_ref.shape[1]
    left = full - wide
    head = lax.broadcasted_iota(jnp.int32, (8, full), 0) < 4
    near = lax.broadcasted_iota(jnp.int32, (8, half), 0) < 4
    for c in range(32):
        g_ref[c * 16 : c * 16 + 16] = peers[c][:, wide:]
    lines = []
    for core in range(2):
        for y in range(8):
            firsts, rests = [], []
            for c in (4 * y + 2 * core, 4 * y + 2 * core + 1):
                v = peers[c][:, :wide].astype(F32)
                firsts.append(jnp.concatenate([v[:8], v[8:, :left]], axis=1))
                rests.append(v[8:, left : left + half])
            even, odd = rests
            low = jnp.where(near, even, pltpu.roll(odd, 4, 0))
            high = jnp.where(near, pltpu.roll(even, 4, 0), odd)
            last = jnp.concatenate([low, high], axis=1)
            turned = pltpu.roll(firsts[1], 4, 0)
            lines += [firsts[0], jnp.where(head, last, turned), jnp.where(head, turned, last)]
    x = jnp.concatenate(lines, axis=0).astype(BF)
    out_ref[...] = dot(x, w_ref[...]).astype(BF)


def grad_body(g_ref, s_ref, w_ref, out_ref):
    w = w_ref[...]
    n = g_ref.shape[0]
    out_ref[:n] = dot(g_ref[...], w).astype(BF)
    s = dot(s_ref[...], w)
    spare = jnp.zeros((out_ref.shape[0] - n - s.shape[0], s.shape[1]), F32)
    out_ref[n:] = jnp.concatenate([s, spare], axis=0).astype(BF)


def scaled_body(a_ref, g_ref, e_ref, scaled_ref, out_ref):
    n = a_ref.shape[0]
    a = a_ref[...].T
    g = g_ref[:n]
    sk = g_ref[n : n + 80]
    odd = lax.broadcasted_iota(jnp.int32, g.shape, 0) % 2
    e = e_ref[...].astype(F32)
    parts = []
    for q in range(2):
        mine = jnp.where(odd == q, g.astype(F32), 0.0).astype(BF)
        s = (dot(a, mine) / e).astype(BF)
        scaled_ref[q] = s
        parts.append(dot(sk, s, 1, 1)[:72])
    to_tiles(jnp.concatenate(parts, axis=0), out_ref, out_ref.shape[1])


def range_body(r_ref, w_ref, out_ref):
    r = from_tiles(r_ref, 4, 9, 7)
    to_tiles(dot(r, w_ref[...], 1, 1), out_ref, 4)


def mapped_slot(t):
    return divmod(t, 6) if t < 42 else (7 + (t - 42) // 3, (t - 42) % 3)


def split3(x):
    hi = x.astype(BF)
    left = x - hi.astype(F32)
    mid = left.astype(BF)
    return hi, mid, (left - mid.astype(F32)).astype(BF)


def mapped_body(r_ref, w_ref, out_ref):
    r = from_tiles(r_ref, 4, 9, 14)
    y = dot(r, w_ref[...]).astype(BF)
    for t in range(69):
        p, s = mapped_slot(t)
        a, g = divmod(t, 7)
        tile = y[a * 16 : a * 16 + 16, g * 128 : g * 128 + 128] if t < 63 else jnp.zeros((16, 128), BF)
        out_ref[p, s] = tile
    wide = r.astype(F32)
    grams = []
    for q in range(2):
        rq = wide[q * 72 : q * 72 + 72].astype(BF)
        g = dot(rq, rq, 1, 1)
        grams.append(jnp.concatenate([g, jnp.zeros((72, 56), F32)], axis=1))
    gram = jnp.concatenate(grams, axis=0)
    for i, part in enumerate(split3(gram)):
        for a in range(9):
            out_ref[7 + a, 3 + i] = part[a * 16 : a * 16 + 16]


def gram_sum_body(x_ref, out_ref):
    total = jnp.sum(x_ref[...].astype(F32), axis=0)
    whole = total[3] + total[4] + total[5]
    plain = lax.axis_index("y") * 2 + lax.axis_index("core") < 7
    parts = split3(whole)
    for i in range(6):
        tile = total[i].astype(BF)
        if i >= 3:
            tile = jnp.where(plain, total[i], parts[i - 3].astype(F32)).astype(BF)
        out_ref[i] = tile


def core_body(m_ref, s_ref, out_ref):
    tiles = [m_ref[mapped_slot(t)] for t in range(63)]
    m = jnp.concatenate(
        [jnp.concatenate(tiles[r * 7 : r * 7 + 7], axis=1) for r in range(9)], axis=0
    ).astype(F32)
    parts = [dot(m[q * 72 : q * 72 + 72].astype(BF), s_ref[q]) for q in range(2)]
    to_tiles(jnp.concatenate(parts, axis=0), out_ref, 2)


def inverse_body(m_ref, out_ref):
    gram = jnp.concatenate(
        [sum(m_ref[7 + a, 3 + i].astype(F32) for i in range(3)) for a in range(9)], axis=0
    )
    rows = lax.broadcasted_iota(jnp.int32, (72, 128), 0)
    lanes = lax.broadcasted_iota(jnp.int32, (72, 128), 1)
    below = lax.broadcasted_iota(jnp.int32, (72, 1), 0)
    eye = jnp.where(rows == lanes, 1.0, 0.0)
    left = [gram[q * 72 : q * 72 + 72] for q in range(2)]
    right = [eye, eye]
    for k in range(72):
        for q in range(2):
            pivot = left[q][k : k + 1]
            f = left[q][:, k : k + 1] / pivot[:, k : k + 1]
            f = jnp.where(below > k, f, 0.0)
            line = right[q][k : k + 1]
            left[q] = left[q] - f * pivot
            right[q] = right[q] - f * line
    for q in range(2):
        d = jnp.sum(jnp.where(rows == lanes, left[q], 0.0), axis=1, keepdims=True)
        out_ref[q] = right[q] / jnp.sqrt(d)


def basis_body(w_ref, r_ref, out_ref):
    r = from_tiles(r_ref, 4, 9, 14).astype(F32)
    for q in range(2):
        w = w_ref[q][:, :72]
        out_ref[q] = dot(w, r[q * 72 : q * 72 + 72], precision=lax.Precision.HIGHEST)


def project_body(c_ref, w_ref, out_ref):
    c = from_tiles(c_ref, 2, 9, 4)
    to_tiles(dot(c, w_ref[...], 1, 1), out_ref, 2)


def final_body(w_ref, p_ref, out_ref):
    p = from_tiles(p_ref, 2, 9, 2).astype(F32)
    for q in range(2):
        w = w_ref[q][:, :72]
        out_ref[q] = dot(w, p[q * 72 : q * 72 + 72], precision=lax.Precision.HIGHEST)


def on_device(acts, grads, basis_in, basis_out, eigen, sketch):
    g = jnp.broadcast_to(grads.reshape(1, 24, 256), (16, 24, 256))
    all_grads = swap(g, ROW).reshape(384, 256)
    g_part = call(grad_body, ((512, 512), BF), all_grads, sketch, basis_out)
    own = swap(g_part.reshape(32, 16, 512), COL)
    joined = call(join_body, ((8, 16, 1920), BF), own, acts.reshape(12, 1792))
    near = swap(joined, "z")
    both = swap(jnp.broadcast_to(near[None], (4, 8, 16, 1920)), "x")
    a_part, g_rot = call(act_body, [((384, 896), BF), ((512, 512), BF)], both, basis_in)
    a_own = summed(summed(a_part.reshape(2, 8, 24, 896), "core"), "y")
    a_rot = lax.all_gather(a_own, ROW).reshape(384, 896)
    scaled, red = call(
        scaled_body, [((2, 896, 512), BF), ((16, 4, 16, 128), BF)], a_rot, g_rot, eigen
    )
    reduced = sum_over(red, ROW)
    span = call(range_body, ((32, 4, 16, 128), BF), reduced, basis_in)
    span = sum_over(span, COL)
    mapped = swap(call(mapped_body, ((16, 6, 16, 128), BF), span, basis_in), ROW)
    mapped = lax.all_gather(call(gram_sum_body, ((6, 16, 128), BF), mapped), ROW)
    core = sum_over(call(core_body, ((32, 2, 16, 128), BF), mapped, scaled), COL)
    inverse = call(inverse_body, ((2, 72, 128), F32), mapped)
    basis = call(basis_body, ((2, 72, 1792), F32), inverse, span)
    proj = sum_over(call(project_body, ((16, 2, 16, 128), BF), core, basis_out), ROW)
    return basis, call(final_body, ((2, 72, 256), F32), inverse, proj)


def solution(mesh):
    split = Mesh(mesh.devices.reshape(8, 2, 8, 4), ("y", "core", "z", "x"))
    return jax.shard_map(
        on_device,
        mesh=split,
        in_specs=(
            P(COL, None, ROW),
            P(ROW, None, COL),
            P(ROW, COL),
            P(COL, ROW),
            P(COL, ROW),
            P(None, COL),
        ),
        out_specs=(P(None, None, ROW), P(None, None, COL)),
        check_vma=False,
    )
```

```python
import functools

import jax
import jax.numpy as jnp
from jax import lax
from jax.experimental import pallas as pl
from jax.experimental.pallas import tpu as pltpu
from jax.sharding import Mesh
from jax.sharding import PartitionSpec as P

COL = ("z", "x")
ROW = ("y", "core")
BF = jnp.bfloat16
F32 = jnp.float32
MIB = 1024 * 1024


def call(body, out, *args, limit=32):
    many = isinstance(out, list)
    shapes = [jax.ShapeDtypeStruct(s, d) for s, d in (out if many else [out])]
    got = pl.pallas_call(
        body,
        out_shape=shapes,
        in_specs=[pl.BlockSpec(memory_space=pltpu.VMEM)] * len(args),
        out_specs=[pl.BlockSpec(memory_space=pltpu.VMEM)] * len(shapes),
        compiler_params=pltpu.CompilerParams(vmem_limit_bytes=limit * MIB),
    )(*args)
    return got if many else got[0]


def swap(x, axes):
    return lax.all_to_all(x, axes, 0, 0, tiled=True)


def dot(a, b, ca=1, cb=0, **kw):
    return lax.dot_general(a, b, (((ca,), (cb,)), ((), ())), preferred_element_type=F32, **kw)


def to_tiles(y, out_ref, slots):
    lanes = y.shape[1] // 128
    count = (y.shape[0] // 16) * lanes
    y = y.astype(BF)
    for t in range(out_ref.shape[0] * slots):
        if t < count:
            r, g = divmod(t, lanes)
            tile = y[r * 16 : r * 16 + 16, g * 128 : g * 128 + 128]
        else:
            tile = jnp.zeros((16, 128), BF)
        out_ref[t // slots, t % slots] = tile


def from_tiles(ref, slots, rows, lanes):
    lines = []
    for r in range(rows):
        at = [divmod(r * lanes + g, slots) for g in range(lanes)]
        lines.append(jnp.concatenate([ref[p, s] for p, s in at], axis=1))
    return jnp.concatenate(lines, axis=0)


def sum_body(x_ref, out_ref):
    total = jnp.sum(x_ref[...].astype(F32), axis=0).astype(BF)
    out_ref[...] = jnp.broadcast_to(total[None], out_ref.shape)


def sum_one_body(x_ref, out_ref):
    out_ref[...] = jnp.sum(x_ref[...].astype(F32), axis=0).astype(BF)


def summed(pieces, axes):
    own = swap(pieces, axes)
    return call(sum_one_body, (own.shape[1:], BF), own)


def add_body(a_ref, b_ref, out_ref):
    out_ref[...] = (a_ref[...].astype(F32) + b_ref[...].astype(F32)).astype(BF)


def sum_over(pieces, axes):
    own = swap(pieces, axes)
    return swap(call(sum_body, (own.shape, BF), own), axes)


def pack_body(x_ref, out_ref):
    x = x_ref[...].astype(F32)
    half = x.shape[1] // 2
    wide = out_ref.shape[2]
    first, rest = x[:8], x[8:]
    rest = jnp.concatenate([rest[:, :half], rest[:, half:]], axis=0)
    spare = jnp.zeros((8, 2 * wide - x.shape[1] - half), F32)
    bottom = jnp.concatenate([first[:, wide:], rest, spare], axis=1)
    packed = jnp.concatenate([first[:, :wide], bottom], axis=0).astype(BF)
    out_ref[...] = jnp.broadcast_to(packed[None], out_ref.shape)


def act_body(x_ref, w_ref, keep_ref, out_ref):
    peers = [x_ref[c % 4, c // 4] for c in range(32)]
    full = w_ref.shape[0]
    half = full // 2
    wide = x_ref.shape[3]
    left = full - wide
    head = lax.broadcasted_iota(jnp.int32, (8, full), 0) < 4
    near = lax.broadcasted_iota(jnp.int32, (8, half), 0) < 4
    lines = []
    for core in range(2):
        for y in range(8):
            firsts, rests = [], []
            for c in (4 * y + 2 * core, 4 * y + 2 * core + 1):
                v = peers[c].astype(F32)
                firsts.append(jnp.concatenate([v[:8], v[8:, :left]], axis=1))
                rests.append(v[8:, left : left + half])
            even, odd = rests
            low = jnp.where(near, even, pltpu.roll(odd, 4, 0))
            high = jnp.where(near, pltpu.roll(even, 4, 0), odd)
            last = jnp.concatenate([low, high], axis=1)
            turned = pltpu.roll(firsts[1], 4, 0)
            lines += [firsts[0], jnp.where(head, last, turned), jnp.where(head, turned, last)]
    x = jnp.concatenate(lines, axis=0).astype(BF)
    y = dot(x, w_ref[...])
    n = out_ref.shape[0]
    first = lax.axis_index("core") == 0
    keep_ref[...] = jnp.where(first, y[:n], y[n:]).astype(BF)
    out_ref[...] = jnp.where(first, y[n:], y[:n]).astype(BF)


def grad_body(g_ref, s_ref, w_ref, out_ref):
    w = w_ref[...]
    n = g_ref.shape[0]
    out_ref[:n] = dot(g_ref[...], w).astype(BF)
    s = dot(s_ref[...], w)
    spare = jnp.zeros((out_ref.shape[0] - n - s.shape[0], s.shape[1]), F32)
    out_ref[n:] = jnp.concatenate([s, spare], axis=0).astype(BF)


def scaled_body(a_ref, g_ref, e_ref, scaled_ref, out_ref):
    n = a_ref.shape[0]
    a = a_ref[...].T
    g = g_ref[:n]
    sk = g_ref[n : n + 80]
    odd = lax.broadcasted_iota(jnp.int32, g.shape, 0) % 2
    e = e_ref[...].astype(F32)
    parts = []
    for q in range(2):
        mine = jnp.where(odd == q, g.astype(F32), 0.0).astype(BF)
        s = (dot(a, mine) / e).astype(BF)
        scaled_ref[q] = s
        parts.append(dot(sk, s, 1, 1)[:72])
    to_tiles(jnp.concatenate(parts, axis=0), out_ref, out_ref.shape[1])


def range_body(r_ref, w_ref, out_ref):
    r = from_tiles(r_ref, 4, 9, 7)
    to_tiles(dot(r, w_ref[...], 1, 1), out_ref, 4)


def mapped_slot(t):
    return divmod(t, 6) if t < 42 else (7 + (t - 42) // 3, (t - 42) % 3)


def split3(x):
    hi = x.astype(BF)
    left = x - hi.astype(F32)
    mid = left.astype(BF)
    return hi, mid, (left - mid.astype(F32)).astype(BF)


def mapped_body(r_ref, w_ref, out_ref):
    r = from_tiles(r_ref, 4, 9, 14)
    y = dot(r, w_ref[...]).astype(BF)
    for t in range(69):
        p, s = mapped_slot(t)
        a, g = divmod(t, 7)
        tile = y[a * 16 : a * 16 + 16, g * 128 : g * 128 + 128] if t < 63 else jnp.zeros((16, 128), BF)
        out_ref[p, s] = tile
    wide = r.astype(F32)
    grams = []
    for q in range(2):
        rq = wide[q * 72 : q * 72 + 72].astype(BF)
        g = dot(rq, rq, 1, 1)
        grams.append(jnp.concatenate([g, jnp.zeros((72, 56), F32)], axis=1))
    gram = jnp.concatenate(grams, axis=0)
    for i, part in enumerate(split3(gram)):
        for a in range(9):
            out_ref[7 + a, 3 + i] = part[a * 16 : a * 16 + 16]


def gram_sum_body(x_ref, out_ref):
    total = jnp.sum(x_ref[...].astype(F32), axis=0)
    whole = total[3] + total[4] + total[5]
    plain = lax.axis_index("y") * 2 + lax.axis_index("core") < 7
    parts = split3(whole)
    for i in range(6):
        tile = total[i].astype(BF)
        if i >= 3:
            tile = jnp.where(plain, total[i], parts[i - 3].astype(F32)).astype(BF)
        out_ref[i] = tile


def core_body(m_ref, s_ref, out_ref):
    tiles = [m_ref[mapped_slot(t)] for t in range(63)]
    m = jnp.concatenate(
        [jnp.concatenate(tiles[r * 7 : r * 7 + 7], axis=1) for r in range(9)], axis=0
    ).astype(F32)
    parts = [dot(m[q * 72 : q * 72 + 72].astype(BF), s_ref[q]) for q in range(2)]
    to_tiles(jnp.concatenate(parts, axis=0), out_ref, 2)


def inverse_body(m_ref, out_ref):
    gram = jnp.concatenate(
        [sum(m_ref[7 + a, 3 + i].astype(F32) for i in range(3)) for a in range(9)], axis=0
    )
    rows = lax.broadcasted_iota(jnp.int32, (72, 128), 0)
    lanes = lax.broadcasted_iota(jnp.int32, (72, 128), 1)
    below = lax.broadcasted_iota(jnp.int32, (72, 1), 0)
    eye = jnp.where(rows == lanes, 1.0, 0.0)
    left = [gram[q * 72 : q * 72 + 72] for q in range(2)]
    right = [eye, eye]
    for k in range(72):
        for q in range(2):
            pivot = left[q][k : k + 1]
            f = left[q][:, k : k + 1] / pivot[:, k : k + 1]
            f = jnp.where(below > k, f, 0.0)
            line = right[q][k : k + 1]
            left[q] = left[q] - f * pivot
            right[q] = right[q] - f * line
    for q in range(2):
        d = jnp.sum(jnp.where(rows == lanes, left[q], 0.0), axis=1, keepdims=True)
        out_ref[q] = right[q] / jnp.sqrt(d)


def basis_body(w_ref, r_ref, out_ref):
    r = from_tiles(r_ref, 4, 9, 14).astype(F32)
    for q in range(2):
        w = w_ref[q][:, :72]
        out_ref[q] = dot(w, r[q * 72 : q * 72 + 72], precision=lax.Precision.HIGHEST)


def project_body(c_ref, w_ref, out_ref):
    c = from_tiles(c_ref, 2, 9, 4)
    to_tiles(dot(c, w_ref[...], 1, 1), out_ref, 2)


def final_body(w_ref, p_ref, out_ref):
    p = from_tiles(p_ref, 2, 9, 2).astype(F32)
    for q in range(2):
        w = w_ref[q][:, :72]
        out_ref[q] = dot(w, p[q * 72 : q * 72 + 72], precision=lax.Precision.HIGHEST)


def on_device(acts, grads, basis_in, basis_out, eigen, sketch):
    packed = call(pack_body, ((8, 16, 1408), BF), acts.reshape(12, 1792))
    near = swap(packed, "z")
    all_grads = lax.all_gather(grads.reshape(24, 256), ROW).reshape(384, 256)
    near, all_grads = lax.optimization_barrier((near, all_grads))
    g_part = call(grad_body, ((512, 512), BF), all_grads, sketch, basis_out)
    both = swap(jnp.broadcast_to(near[None], (4, 8, 16, 1408)), "x")
    both, g_part = lax.optimization_barrier((both, g_part))
    g_own = summed(g_part.reshape(32, 16, 512), COL)
    keep, give = call(act_body, [((192, 896), BF), ((192, 896), BF)], both, basis_in)
    give = lax.ppermute(give, "core", [(0, 1), (1, 0)])
    a_pair = call(add_body, ((192, 896), BF), keep, give)
    a_pair, g_own = lax.optimization_barrier((a_pair, g_own))
    a_own = summed(a_pair.reshape(8, 24, 896), "y")
    a_own, g_own = lax.optimization_barrier((a_own, g_own))
    g_rot = swap(jnp.broadcast_to(g_own[None], (32, 16, 512)), COL).reshape(512, 512)
    a_rot = lax.all_gather(a_own, ROW).reshape(384, 896)
    scaled, red = call(
        scaled_body, [((2, 896, 512), BF), ((16, 4, 16, 128), BF)], a_rot, g_rot, eigen
    )
    reduced = sum_over(red, ROW)
    span = call(range_body, ((32, 4, 16, 128), BF), reduced, basis_in)
    span = sum_over(span, COL)
    mapped = swap(call(mapped_body, ((16, 6, 16, 128), BF), span, basis_in), ROW)
    mapped = lax.all_gather(call(gram_sum_body, ((6, 16, 128), BF), mapped), ROW)
    core = sum_over(call(core_body, ((32, 2, 16, 128), BF), mapped, scaled), COL)
    inverse = call(inverse_body, ((2, 72, 128), F32), mapped)
    basis = call(basis_body, ((2, 72, 1792), F32), inverse, span)
    proj = sum_over(call(project_body, ((16, 2, 16, 128), BF), core, basis_out), ROW)
    return basis, call(final_body, ((2, 72, 256), F32), inverse, proj)


def solution(mesh):
    split = Mesh(mesh.devices.reshape(8, 2, 8, 4), ("y", "core", "z", "x"))
    return jax.shard_map(
        on_device,
        mesh=split,
        in_specs=(
            P(COL, None, ROW),
            P(ROW, None, COL),
            P(ROW, COL),
            P(COL, ROW),
            P(COL, ROW),
            P(None, COL),
        ),
        out_specs=(P(None, None, ROW), P(None, None, COL)),
        check_vma=False,
    )
```

```python
import functools

import jax
import jax.numpy as jnp
from jax import lax
from jax.experimental import pallas as pl
from jax.experimental.pallas import tpu as pltpu
from jax.sharding import Mesh
from jax.sharding import PartitionSpec as P

COL = ("z", "x")
ROW = ("y", "core")
BF = jnp.bfloat16
F32 = jnp.float32
MIB = 1024 * 1024


def call(body, out, *args, limit=32):
    many = isinstance(out, list)
    shapes = [jax.ShapeDtypeStruct(s, d) for s, d in (out if many else [out])]
    got = pl.pallas_call(
        body,
        out_shape=shapes,
        in_specs=[pl.BlockSpec(memory_space=pltpu.VMEM)] * len(args),
        out_specs=[pl.BlockSpec(memory_space=pltpu.VMEM)] * len(shapes),
        compiler_params=pltpu.CompilerParams(vmem_limit_bytes=limit * MIB),
    )(*args)
    return got if many else got[0]


def swap(x, axes):
    return lax.all_to_all(x, axes, 0, 0, tiled=True)


def dot(a, b, ca=1, cb=0, **kw):
    return lax.dot_general(a, b, (((ca,), (cb,)), ((), ())), preferred_element_type=F32, **kw)


def to_tiles(y, out_ref):
    slots, high = out_ref.shape[1:3]
    lanes = y.shape[1] // 128
    count = (y.shape[0] // high) * lanes
    for t in range(out_ref.shape[0] * slots):
        if t < count:
            r, g = divmod(t, lanes)
            tile = y[r * high : r * high + high, g * 128 : g * 128 + 128]
        else:
            tile = jnp.zeros((high, 128), F32)
        out_ref[t // slots, t % slots] = tile.astype(BF)


def from_tiles(ref, lanes):
    slots, high = ref.shape[1:3]
    lines = []
    for r in range(144 // high):
        at = [divmod(r * lanes + g, slots) for g in range(lanes)]
        lines.append(jnp.concatenate([ref[p, s].astype(F32) for p, s in at], axis=1))
    return jnp.concatenate(lines, axis=0)


def sum_body(x_ref, out_ref):
    total = jnp.sum(x_ref[...].astype(F32), axis=0).astype(BF)
    out_ref[...] = jnp.broadcast_to(total[None], out_ref.shape)


def sum_one_body(x_ref, out_ref):
    out_ref[...] = jnp.sum(x_ref[...].astype(F32), axis=0).astype(BF)


def summed(pieces, axes):
    own = swap(pieces, axes)
    return call(sum_one_body, (own.shape[1:], BF), own)


def add_body(a_ref, b_ref, out_ref):
    out_ref[...] = (a_ref[...].astype(F32) + b_ref[...].astype(F32)).astype(BF)


def sum_over(pieces, axes):
    own = swap(pieces, axes)
    return swap(call(sum_body, (own.shape, BF), own), axes)


def pack_body(x_ref, out_ref):
    x = x_ref[...].astype(F32)
    half = x.shape[1] // 2
    wide = out_ref.shape[2]
    first, rest = x[:8], x[8:]
    rest = jnp.concatenate([rest[:, :half], rest[:, half:]], axis=0)
    spare = jnp.zeros((8, 2 * wide - x.shape[1] - half), F32)
    bottom = jnp.concatenate([first[:, wide:], rest, spare], axis=1)
    packed = jnp.concatenate([first[:, :wide], bottom], axis=0).astype(BF)
    out_ref[...] = jnp.broadcast_to(packed[None], out_ref.shape)


def act_body(x_ref, w_ref, keep_ref, out_ref):
    peers = [x_ref[c % 4, c // 4] for c in range(32)]
    full = w_ref.shape[0]
    half = full // 2
    wide = x_ref.shape[3]
    left = full - wide
    head = lax.broadcasted_iota(jnp.int32, (8, full), 0) < 4
    near = lax.broadcasted_iota(jnp.int32, (8, half), 0) < 4
    lines = []
    for core in range(2):
        for y in range(8):
            firsts, rests = [], []
            for c in (4 * y + 2 * core, 4 * y + 2 * core + 1):
                v = peers[c].astype(F32)
                firsts.append(jnp.concatenate([v[:8], v[8:, :left]], axis=1))
                rests.append(v[8:, left : left + half])
            even, odd = rests
            low = jnp.where(near, even, pltpu.roll(odd, 4, 0))
            high = jnp.where(near, pltpu.roll(even, 4, 0), odd)
            last = jnp.concatenate([low, high], axis=1)
            turned = pltpu.roll(firsts[1], 4, 0)
            lines += [firsts[0], jnp.where(head, last, turned), jnp.where(head, turned, last)]
    x = jnp.concatenate(lines, axis=0).astype(BF)
    y = dot(x, w_ref[...])
    n = out_ref.shape[0]
    first = lax.axis_index("core") == 0
    keep_ref[...] = jnp.where(first, y[:n], y[n:]).astype(BF)
    out_ref[...] = jnp.where(first, y[n:], y[:n]).astype(BF)


def grad_body(g_ref, s_ref, w_ref, out_ref):
    w = w_ref[...]
    n = g_ref.shape[0]
    out_ref[:n] = dot(g_ref[...], w).astype(BF)
    s = dot(s_ref[...], w)
    spare = jnp.zeros((out_ref.shape[0] - n - s.shape[0], s.shape[1]), F32)
    out_ref[n:] = jnp.concatenate([s, spare], axis=0).astype(BF)


def scaled_body(a_ref, g_ref, e_ref, scaled_ref, out_ref):
    n = a_ref.shape[0]
    a = a_ref[...].T
    g = g_ref[:n]
    sk = g_ref[n : n + 80]
    odd = lax.broadcasted_iota(jnp.int32, g.shape, 0) % 2
    e = e_ref[...].astype(F32)
    parts = []
    for q in range(2):
        mine = jnp.where(odd == q, g.astype(F32), 0.0).astype(BF)
        s = (dot(a, mine) / e).astype(BF)
        scaled_ref[q] = s
        parts.append(dot(sk, s, 1, 1)[:72])
    to_tiles(jnp.concatenate(parts, axis=0), out_ref)


def range_body(r_ref, w_ref, out_ref):
    r = from_tiles(r_ref, 7).astype(BF)
    to_tiles(dot(r, w_ref[...], 1, 1), out_ref)


def mapped_body(r_ref, w_ref, out_ref, gram_ref):
    r = from_tiles(r_ref, 14)
    to_tiles(dot(r.astype(BF), w_ref[...]), out_ref)
    for q in range(2):
        rq = r[q * 72 : q * 72 + 72].astype(BF)
        gram_ref[q] = dot(rq, rq, 1, 1)


def core_body(m_ref, s_ref, out_ref):
    m = from_tiles(m_ref, 7)
    parts = [dot(m[q * 72 : q * 72 + 72].astype(BF), s_ref[q]) for q in range(2)]
    to_tiles(jnp.concatenate(parts, axis=0), out_ref)


def inverse_body(m_ref, out_ref):
    rows = lax.broadcasted_iota(jnp.int32, (72, 128), 0)
    lanes = lax.broadcasted_iota(jnp.int32, (72, 128), 1)
    below = lax.broadcasted_iota(jnp.int32, (72, 1), 0)
    eye = jnp.where(rows == lanes, 1.0, 0.0)
    spare = jnp.zeros((72, 56), F32)
    left = [jnp.concatenate([jnp.sum(m_ref[:, q], axis=0), spare], axis=1) for q in range(2)]
    right = [eye, eye]
    for k in range(72):
        for q in range(2):
            pivot = left[q][k : k + 1]
            f = left[q][:, k : k + 1] / pivot[:, k : k + 1]
            f = jnp.where(below > k, f, 0.0)
            line = right[q][k : k + 1]
            left[q] = left[q] - f * pivot
            right[q] = right[q] - f * line
    for q in range(2):
        d = jnp.sum(jnp.where(rows == lanes, left[q], 0.0), axis=1, keepdims=True)
        out_ref[q] = right[q] / jnp.sqrt(d)


def basis_body(w_ref, r_ref, out_ref):
    r = from_tiles(r_ref, 14)
    for q in range(2):
        w = w_ref[q][:, :72]
        out_ref[q] = dot(w, r[q * 72 : q * 72 + 72], precision=lax.Precision.HIGHEST)


def project_body(c_ref, w_ref, out_ref):
    c = from_tiles(c_ref, 4).astype(BF)
    out_ref[...] = dot(c, w_ref[...], 1, 1).astype(BF)


def query_body(p_ref, out_ref):
    p = p_ref[0].astype(F32) + p_ref[1].astype(F32)
    mine = jnp.where(lax.axis_index("core") == 0, p[:72], p[72:]).astype(BF)
    out_ref[...] = jnp.broadcast_to(mine[None], out_ref.shape)


def final_body(w_ref, p_ref, out_ref):
    p = jnp.sum(p_ref[...].astype(F32), axis=0)
    w = jnp.where(lax.axis_index("core") == 0, w_ref[0], w_ref[1])[:, :72]
    out_ref[...] = dot(w, p, precision=lax.Precision.HIGHEST)


def on_device(acts, grads, basis_in, basis_out, eigen, sketch):
    packed = call(pack_body, ((8, 16, 1408), BF), acts.reshape(12, 1792))
    near = swap(packed, "z")
    near, own_grads = lax.optimization_barrier((near, grads.reshape(24, 256)))
    all_grads = lax.all_gather(own_grads, ROW).reshape(384, 256)
    g_part = call(grad_body, ((512, 512), BF), all_grads, sketch, basis_out)
    both = swap(jnp.broadcast_to(near[None], (4, 8, 16, 1408)), "x")
    both, g_part = lax.optimization_barrier((both, g_part))
    g_own = summed(g_part.reshape(32, 16, 512), COL)
    keep, give = call(act_body, [((192, 896), BF), ((192, 896), BF)], both, basis_in)
    give = lax.ppermute(give, "core", [(0, 1), (1, 0)])
    a_pair = call(add_body, ((192, 896), BF), keep, give)
    a_pair, g_own = lax.optimization_barrier((a_pair, g_own))
    a_own = summed(a_pair.reshape(8, 24, 896), "y")
    a_own, g_own = lax.optimization_barrier((a_own, g_own))
    g_rot = swap(jnp.broadcast_to(g_own[None], (32, 16, 512)), COL).reshape(512, 512)
    a_rot = lax.all_gather(a_own, ROW).reshape(384, 896)
    scaled, red = call(
        scaled_body, [((2, 896, 512), BF), ((16, 4, 16, 128), BF)], a_rot, g_rot, eigen
    )
    reduced = sum_over(red, ROW)
    span = call(range_body, ((32, 4, 16, 128), BF), reduced, basis_in)
    span = sum_over(span, COL)
    pieces, gram = call(
        mapped_body, [((16, 4, 16, 128), BF), ((2, 72, 72), F32)], span, basis_in
    )
    mapped = sum_over(pieces, ROW)
    core = call(core_body, ((32, 3, 8, 128), BF), mapped, scaled)
    core, gram = lax.optimization_barrier((core, gram))
    grams = lax.all_gather(gram, ROW)
    core, grams = lax.optimization_barrier((summed(core, COL), grams))
    core = swap(jnp.broadcast_to(core[None], (32, 3, 8, 128)), COL)
    inverse = call(inverse_body, ((2, 72, 128), F32), grams)
    basis = call(basis_body, ((2, 72, 1792), F32), inverse, span)
    part = call(project_body, ((144, 256), BF), core, basis_out)
    mine = call(query_body, ((8, 72, 256), BF), lax.all_gather(part, "core"))
    mine = call(final_body, ((72, 256), F32), inverse, swap(mine, "y"))
    return basis, lax.all_gather(mine, "core")


def solution(mesh):
    split = Mesh(mesh.devices.reshape(8, 2, 8, 4), ("y", "core", "z", "x"))
    return jax.shard_map(
        on_device,
        mesh=split,
        in_specs=(
            P(COL, None, ROW),
            P(ROW, None, COL),
            P(ROW, COL),
            P(COL, ROW),
            P(COL, ROW),
            P(None, COL),
        ),
        out_specs=(P(None, None, ROW), P(None, None, COL)),
        check_vma=False,
    )
```

```python
import jax
import jax.numpy as jnp
import numpy as np
from jax import lax
from jax.experimental import pallas as pl
from jax.experimental.pallas import tpu as pltpu
from jax.sharding import Mesh
from jax.sharding import PartitionSpec as P

COL = ("z", "x")
ROW = ("y", "core")
BF = jnp.bfloat16
F32 = jnp.float32
MIB = 1024 * 1024


def call(body, out, *args, limit=40):
    many = isinstance(out, list)
    shapes = [jax.ShapeDtypeStruct(s, d) for s, d in (out if many else [out])]
    got = pl.pallas_call(
        body,
        out_shape=shapes,
        in_specs=[pl.BlockSpec(memory_space=pltpu.VMEM)] * len(args),
        out_specs=[pl.BlockSpec(memory_space=pltpu.VMEM)] * len(shapes),
        compiler_params=pltpu.CompilerParams(vmem_limit_bytes=limit * MIB),
    )(*args)
    return got if many else got[0]


def swap(x, axes):
    return lax.all_to_all(x, axes, 0, 0, tiled=True)


def from_sibling(x):
    return lax.ppermute(x, "core", [(0, 1), (1, 0)])


def dot(a, b, ca=1, cb=0, **kw):
    return lax.dot_general(a, b, (((ca,), (cb,)), ((), ())), preferred_element_type=F32, **kw)


def to_tiles(y, out_ref, slots=None):
    slots = slots or out_ref.shape[1]
    lanes = y.shape[1] // 128
    count = (y.shape[0] // 8) * lanes
    for t in range(out_ref.shape[0] * slots):
        if t < count:
            r, g = divmod(t, lanes)
            tile = y[r * 8 : r * 8 + 8, g * 128 : g * 128 + 128]
        else:
            tile = jnp.zeros((8, 128), F32)
        out_ref[t // slots, t % slots] = tile.astype(BF)


def from_tiles(ref, lanes, rows=72, slots=None):
    slots = slots or ref.shape[1]
    lines = []
    for r in range(rows // 8):
        at = [divmod(r * lanes + g, slots) for g in range(lanes)]
        lines.append(jnp.concatenate([ref[p, s].astype(F32) for p, s in at], axis=1))
    return jnp.concatenate(lines, axis=0)


def sum_one_body(x_ref, out_ref):
    out_ref[...] = jnp.sum(x_ref[...].astype(F32), axis=0).astype(BF)


def summed(pieces, axes):
    own = swap(pieces, axes)
    return call(sum_one_body, (own.shape[1:], BF), own)


def sum_body(x_ref, out_ref):
    total = jnp.sum(x_ref[...].astype(F32), axis=0).astype(BF)
    out_ref[...] = jnp.broadcast_to(total[None], out_ref.shape)


def sum_over(pieces, axes):
    own = swap(pieces, axes)
    return swap(call(sum_body, (own.shape, BF), own), axes)


def picked(rows, x):
    lanes = lax.broadcasted_iota(jnp.int32, (rows.shape[0], x.shape[0]), 1)
    return dot(jnp.where(lanes == rows, 1.0, 0.0).astype(BF), x).astype(BF)


def pack_body(x_ref, out_ref):
    core = lax.axis_index("core")
    t = lax.broadcasted_iota(jnp.int32, (8, 1), 0)
    x = x_ref[...]
    parts = []
    for other in range(2):
        at = jnp.where(core == other, 0, 16) + 2 * t + core
        parts.append(picked(jnp.where(t < 6, at, -1), x))
    packed = jnp.concatenate(parts, axis=1)
    out_ref[...] = jnp.broadcast_to(packed[None], out_ref.shape)


def dense_body(rows_ref, x_ref, out_ref):
    y = picked(rows_ref[...], x_ref[...])
    out_ref[...] = jnp.broadcast_to(y[None], out_ref.shape)


def act_body(x_ref, w_ref, v_ref, out_ref):
    n = w_ref.shape[0]
    y = dot(x_ref[:, :n], w_ref[...]) + dot(x_ref[:, n:], v_ref[...])
    out_ref[...] = y.astype(BF)


def grad_body(rows_ref, g_ref, s_ref, w_ref, v_ref, out_ref):
    g = picked(rows_ref[...] + lax.axis_index("core"), g_ref[...])
    s = s_ref[...]
    w, v = w_ref[...], v_ref[...]
    top = jnp.concatenate([dot(g, w), dot(g, v)], axis=1)
    low = jnp.concatenate([dot(s, w), dot(s, v)], axis=1)
    to_tiles(jnp.concatenate([top, low], axis=0), out_ref)


def scaled_body(a_ref, g_ref, e_ref, f_ref, scaled_ref, out_ref):
    core = lax.axis_index("core")
    a = jnp.concatenate([a_ref[y, core].astype(F32) for y in range(8)], axis=0).astype(BF)
    g = from_tiles(g_ref, 8, 264)
    both = dot(a.T, g[:192].astype(BF))
    n = e_ref.shape[1]
    left = (both[:, :n] / e_ref[...].astype(F32)).astype(BF)
    right = (both[:, n:] / f_ref[...].astype(F32)).astype(BF)
    s = jnp.concatenate([left, right], axis=1)
    scaled_ref[...] = s
    to_tiles(dot(g[192:].astype(BF), s, 1, 1), out_ref)


def range_body(r_ref, w_ref, v_ref, out_ref):
    r = from_tiles(r_ref, 7).astype(BF)
    both = [dot(r, w_ref[...], 1, 1), dot(r, v_ref[...], 1, 1)]
    to_tiles(jnp.concatenate(both, axis=1), out_ref)


def split3(x):
    hi = x.astype(BF)
    left = x - hi.astype(F32)
    mid = left.astype(BF)
    return hi, mid, (left - mid.astype(F32)).astype(BF)


def gram_at(g):
    return (g, 9) if g < 8 else (7, 6)


def mapped_body(r_ref, w_ref, v_ref, out_ref, keep_ref, give_ref):
    r = from_tiles(r_ref, 28).astype(BF)
    n = w_ref.shape[0]
    keep_ref[...] = r[:, :n]
    give_ref[...] = r[:, n:]
    to_tiles(dot(r[:, :n], w_ref[...]) + dot(r[:, n:], v_ref[...]), out_ref, 9)
    gram = jnp.concatenate([dot(r, r, 1, 1), jnp.zeros((72, 56), F32)], axis=1)
    for g in range(9):
        p, s = gram_at(g)
        for i, part in enumerate(split3(gram[g * 8 : g * 8 + 8])):
            out_ref[p, s + i] = part


def gram_sum_body(x_ref, out_ref):
    total = jnp.sum(x_ref[...].astype(F32), axis=0)
    last = lax.axis_index("y") == 7
    parts = split3(total[9] + total[10] + total[11])
    spare = split3(total[6] + total[7] + total[8])
    for i in range(12):
        tile = total[i].astype(BF)
        if i >= 9:
            tile = parts[i - 9]
        elif i >= 6:
            tile = jnp.where(last, spare[i - 6].astype(F32), total[i]).astype(BF)
        out_ref[:, i] = jnp.broadcast_to(tile[None], (out_ref.shape[0], 8, 128))


def core_body(m_ref, s_ref, out_ref):
    m = from_tiles(m_ref, 7, slots=9).astype(BF)
    to_tiles(dot(m, s_ref[...]), out_ref)


def inverse_body(m_ref, out_ref):
    tiles = []
    for g in range(9):
        p, s = gram_at(g)
        tiles.append(sum(m_ref[p, s + i].astype(F32) for i in range(3)))
    left = jnp.concatenate(tiles, axis=0)
    rows = lax.broadcasted_iota(jnp.int32, (72, 128), 0)
    lanes = lax.broadcasted_iota(jnp.int32, (72, 128), 1)
    below = lax.broadcasted_iota(jnp.int32, (72, 1), 0)
    right = jnp.where(rows == lanes, 1.0, 0.0)
    for k in range(72):
        pivot = left[k : k + 1]
        f = left[:, k : k + 1] / pivot[:, k : k + 1]
        f = jnp.where(below > k, f, 0.0)
        line = right[k : k + 1]
        left = left - f * pivot
        right = right - f * line
    d = jnp.sum(jnp.where(rows == lanes, left, 0.0), axis=1, keepdims=True)
    out_ref[...] = right / jnp.sqrt(d)


def basis_body(w_ref, keep_ref, got_ref, out_ref):
    core = lax.axis_index("core")
    for q, ref in ((core, keep_ref), (1 - core, got_ref)):
        w = w_ref[q][:, :72]
        out_ref[q] = dot(w, ref[...].astype(F32), precision=lax.Precision.HIGHEST)


def project_body(c_ref, w_ref, v_ref, out_ref):
    c = from_tiles(c_ref, 8).astype(BF)
    n = w_ref.shape[1]
    y = dot(c[:, :n], w_ref[...], 1, 1) + dot(c[:, n:], v_ref[...], 1, 1)
    out_ref[...] = jnp.broadcast_to(y.astype(BF)[None], out_ref.shape)


def final_body(w_ref, p_ref, out_ref):
    p = jnp.sum(p_ref[...].astype(F32), axis=0)
    out_ref[...] = dot(w_ref[...][:, :72], p, precision=lax.Precision.HIGHEST)


DENSE = np.array([[8 * z + t] for z in range(8) for t in range(6)], np.int32)
TOKENS = np.array(
    [[2 * ((z * 4 + x) * 6 + t)] for x in range(4) for z in range(8) for t in range(6)], np.int32
)


def on_device(acts, grads, basis_in, basis_out, eigen, sketch):
    lines = jnp.pad(acts.reshape(12, 1792), ((0, 4), (0, 0)))
    lines = lax.all_gather(lines, "core").reshape(32, 1792)
    packed = call(pack_body, ((8, 8, 3584), BF), lines)
    packed, away = lax.optimization_barrier((packed, (basis_in, basis_out, eigen)))
    far_in, far_out, far_eigen = [from_sibling(w) for w in away]
    near = swap(packed, "z").reshape(64, 3584)
    near, own_grads = lax.optimization_barrier((near, grads.reshape(24, 256)))
    dense = call(dense_body, ((4, 48, 3584), BF), jnp.asarray(DENSE), near)
    all_grads = lax.all_gather(own_grads, ROW).reshape(384, 256)
    g_part = call(
        grad_body, ((32, 9, 8, 128), BF),
        jnp.asarray(TOKENS), all_grads, sketch, basis_out, far_out,
    )
    both = swap(dense, "x").reshape(192, 3584)
    both, g_part = lax.optimization_barrier((both, g_part))
    g_own = summed(g_part, COL)
    a_part = call(act_body, ((192, 896), BF), both, basis_in, far_in)
    a_part, g_own = lax.optimization_barrier((a_part, g_own))
    a_own = summed(a_part.reshape(8, 24, 896), "y")
    a_own, g_own = lax.optimization_barrier((a_own, g_own))
    g_rot = swap(jnp.broadcast_to(g_own[None], (32, 9, 8, 128)), COL)
    a_rot = lax.all_gather(a_own, ROW).reshape(8, 2, 24, 896)
    scaled, red = call(
        scaled_body, [((896, 1024), BF), ((8, 8, 8, 128), BF)], a_rot, g_rot, eigen, far_eigen
    )
    reduced = sum_over(red, "y")
    span = sum_over(call(range_body, ((32, 8, 8, 128), BF), reduced, basis_in, far_in), COL)
    mapped, keep, give = call(
        mapped_body,
        [((8, 12, 8, 128), BF), ((72, 1792), BF), ((72, 1792), BF)],
        span, basis_in, far_in,
    )
    mapped = swap(call(gram_sum_body, ((8, 12, 8, 128), BF), swap(mapped, "y")), "y")
    core = sum_over(call(core_body, ((32, 3, 8, 128), BF), mapped, scaled), COL)
    part = call(project_body, ((8, 72, 256), BF), core, basis_out, far_out)
    inverse = call(inverse_body, ((72, 128), F32), mapped)
    basis = call(
        basis_body, ((2, 72, 1792), F32),
        lax.all_gather(inverse, "core"), keep, from_sibling(give),
    )
    mine = call(final_body, ((72, 256), F32), inverse, swap(part, "y"))
    return basis, lax.all_gather(mine, "core")


def solution(mesh):
    split = Mesh(mesh.devices.reshape(8, 2, 8, 4), ("y", "core", "z", "x"))
    return jax.shard_map(
        on_device,
        mesh=split,
        in_specs=(
            P(COL, None, ROW),
            P(ROW, None, COL),
            P(ROW, COL),
            P(COL, ROW),
            P(COL, ROW),
            P(None, COL),
        ),
        out_specs=(P(None, None, ROW), P(None, None, COL)),
        check_vma=False,
    )
```

```python
import jax
import jax.numpy as jnp
from jax import lax
from jax.experimental import pallas as pl
from jax.experimental.pallas import tpu as pltpu
from jax.sharding import Mesh
from jax.sharding import PartitionSpec as P

COL = ("z", "x")
ROW = ("y", "core")
BF = jnp.bfloat16
F32 = jnp.float32
MIB = 1024 * 1024


def call(body, out, *args, limit=32):
    many = isinstance(out, list)
    shapes = [jax.ShapeDtypeStruct(s, d) for s, d in (out if many else [out])]
    got = pl.pallas_call(
        body,
        out_shape=shapes,
        in_specs=[pl.BlockSpec(memory_space=pltpu.VMEM)] * len(args),
        out_specs=[pl.BlockSpec(memory_space=pltpu.VMEM)] * len(shapes),
        compiler_params=pltpu.CompilerParams(vmem_limit_bytes=limit * MIB),
    )(*args)
    return got if many else got[0]


def swap(x, axes):
    return lax.all_to_all(x, axes, 0, 0, tiled=True)


def from_sibling(x):
    return lax.ppermute(x, "core", [(0, 1), (1, 0)])


def dot(a, b, ca=1, cb=0, **kw):
    return lax.dot_general(a, b, (((ca,), (cb,)), ((), ())), preferred_element_type=F32, **kw)


def to_tiles(y, out_ref, slots=None):
    slots = slots or out_ref.shape[1]
    lanes = y.shape[1] // 128
    count = (y.shape[0] // 8) * lanes
    for t in range(out_ref.shape[0] * slots):
        if t < count:
            r, g = divmod(t, lanes)
            tile = y[r * 8 : r * 8 + 8, g * 128 : g * 128 + 128]
        else:
            tile = jnp.zeros((8, 128), F32)
        out_ref[t // slots, t % slots] = tile.astype(BF)


def to_flat_tiles(y, out_ref):
    lanes = y.shape[1] // 128
    count = (y.shape[0] // 8) * lanes

    def tile(t):
        r, g = divmod(t, lanes)
        return y[r * 8 : r * 8 + 8, g * 128 : g * 128 + 128] if t < count else jnp.zeros((8, 128), F32)

    for t in range(0, out_ref.shape[0] // 8, 2):
        pair = jnp.concatenate([tile(t), tile(t + 1)], axis=0)
        out_ref[t * 8 : t * 8 + 16] = pair.astype(BF)


def from_tiles(ref, lanes, rows=72, slots=None):
    slots = slots or ref.shape[1]
    lines = []
    for r in range(rows // 8):
        at = [divmod(r * lanes + g, slots) for g in range(lanes)]
        lines.append(jnp.concatenate([ref[p, s].astype(F32) for p, s in at], axis=1))
    return jnp.concatenate(lines, axis=0)


def sum_one_body(x_ref, out_ref):
    out_ref[...] = jnp.sum(x_ref[...].astype(F32), axis=0).astype(BF)


def summed(pieces, axes):
    own = swap(pieces, axes)
    return call(sum_one_body, (own.shape[1:], BF), own)


def sum_body(x_ref, out_ref):
    total = jnp.sum(x_ref[...].astype(F32), axis=0).astype(BF)
    out_ref[...] = jnp.broadcast_to(total[None], out_ref.shape)


def sum_flat_body(x_ref, out_ref):
    total = jnp.sum(x_ref[...].astype(F32), axis=0).reshape(-1, 128)
    peers = jnp.broadcast_to(total[None], (x_ref.shape[0], *total.shape))
    out_ref[...] = peers.reshape(out_ref.shape).astype(BF)


def sum_over(pieces, axes):
    own = swap(pieces, axes)
    return swap(call(sum_body, (own.shape, BF), own), axes)


def picked(n, to, x):
    rows = lax.broadcasted_iota(jnp.int32, (n, x.shape[0]), 0)
    return dot(jnp.where(rows == to, 1.0, 0.0).astype(BF), x).astype(BF)


def row_numbers(n):
    return lax.broadcasted_iota(jnp.int32, (1, n), 1)


def pack_body(x_ref, out_ref):
    core = lax.axis_index("core")
    m = row_numbers(32)
    token = (m & 15) >> 1
    parts = []
    for other in range(2):
        block = core if other == 0 else 1 - core
        mine = jnp.logical_and((m >> 4) == block, (m & 1) == core)
        parts.append(picked(8, jnp.where(mine, token, -1), x_ref[...]))
    packed = jnp.concatenate(parts, axis=1).astype(F32)
    peers = jnp.broadcast_to(packed[None], (8, *packed.shape))
    out_ref[...] = peers.reshape(out_ref.shape).astype(BF)


def dense_body(x_ref, out_ref):
    m = row_numbers(64)
    token = m & 7
    y = picked(48, jnp.where(token < 6, (m >> 3) * 6 + token, -1), x_ref[...])
    out_ref[...] = jnp.broadcast_to(y[None], out_ref.shape)


def act_body(x_ref, w_ref, v_ref, out_ref):
    n = w_ref.shape[0]
    y = dot(x_ref[:, :n], w_ref[...]) + dot(x_ref[:, n:], v_ref[...])
    out_ref[...] = y.astype(BF)


def grad_body(g_ref, s_ref, w_ref, v_ref, out_ref):
    m = row_numbers(384)
    token = m >> 1
    peer = jnp.floor((token.astype(F32) + 0.5) * (1.0 / 6.0)).astype(jnp.int32)
    to = (peer & 3) * 48 + (peer >> 2) * 6 + token - peer * 6
    g = picked(192, jnp.where((m & 1) == lax.axis_index("core"), to, -1), g_ref[...])
    s = s_ref[...]
    w, v = w_ref[...], v_ref[...]
    top = jnp.concatenate([dot(g, w), dot(g, v)], axis=1)
    low = jnp.concatenate([dot(s, w), dot(s, v)], axis=1)
    to_flat_tiles(jnp.concatenate([top, low], axis=0), out_ref)


def scaled_body(a_ref, g_ref, e_ref, f_ref, scaled_ref, out_ref):
    core = lax.axis_index("core")
    a = jnp.concatenate([a_ref[y, core].astype(F32) for y in range(8)], axis=0).astype(BF)
    g = from_tiles(g_ref, 8, 264)
    both = dot(a.T, g[:192].astype(BF))
    n = e_ref.shape[1]
    left = (both[:, :n] / e_ref[...].astype(F32)).astype(BF)
    right = (both[:, n:] / f_ref[...].astype(F32)).astype(BF)
    s = jnp.concatenate([left, right], axis=1)
    scaled_ref[...] = s
    to_tiles(dot(g[192:].astype(BF), s, 1, 1), out_ref)


def range_body(r_ref, w_ref, v_ref, out_ref):
    r = from_tiles(r_ref, 7).astype(BF)
    both = [dot(r, w_ref[...], 1, 1), dot(r, v_ref[...], 1, 1)]
    to_tiles(jnp.concatenate(both, axis=1), out_ref)


def split3(x):
    hi = x.astype(BF)
    left = x - hi.astype(F32)
    mid = left.astype(BF)
    return hi, mid, (left - mid.astype(F32)).astype(BF)


def gram_at(g):
    return (g, 9) if g < 8 else (7, 6)


def mapped_body(r_ref, w_ref, v_ref, out_ref, keep_ref, give_ref):
    r = from_tiles(r_ref, 28).astype(BF)
    n = w_ref.shape[0]
    keep_ref[...] = r[:, :n]
    give_ref[...] = r[:, n:]
    to_tiles(dot(r[:, :n], w_ref[...]) + dot(r[:, n:], v_ref[...]), out_ref, 9)
    gram = jnp.concatenate([dot(r, r, 1, 1), jnp.zeros((72, 56), F32)], axis=1)
    for g in range(9):
        p, s = gram_at(g)
        for i, part in enumerate(split3(gram[g * 8 : g * 8 + 8])):
            out_ref[p, s + i] = part


def gram_sum_body(x_ref, out_ref):
    total = jnp.sum(x_ref[...].astype(F32), axis=0)
    last = lax.axis_index("y") == 7
    parts = split3(total[9] + total[10] + total[11])
    spare = split3(total[6] + total[7] + total[8])
    for i in range(12):
        tile = total[i].astype(BF)
        if i >= 9:
            tile = parts[i - 9]
        elif i >= 6:
            tile = jnp.where(last, spare[i - 6].astype(F32), total[i]).astype(BF)
        out_ref[:, i] = jnp.broadcast_to(tile[None], (out_ref.shape[0], 8, 128))


def core_body(m_ref, s_ref, out_ref):
    m = from_tiles(m_ref, 7, slots=9).astype(BF)
    to_flat_tiles(dot(m, s_ref[...]), out_ref)


def inverse_body(m_ref, out_ref):
    tiles = []
    for g in range(9):
        p, s = gram_at(g)
        tiles.append(sum(m_ref[p, s + i].astype(F32) for i in range(3)))
    left = jnp.concatenate(tiles, axis=0)
    rows = lax.broadcasted_iota(jnp.int32, (72, 128), 0)
    lanes = lax.broadcasted_iota(jnp.int32, (72, 128), 1)
    below = lax.broadcasted_iota(jnp.int32, (72, 1), 0)
    right = jnp.where(rows == lanes, 1.0, 0.0)
    for k in range(72):
        pivot = left[k : k + 1]
        f = left[:, k : k + 1] / pivot[:, k : k + 1]
        f = jnp.where(below > k, f, 0.0)
        line = right[k : k + 1]
        left = left - f * pivot
        right = right - f * line
    d = jnp.sum(jnp.where(rows == lanes, left, 0.0), axis=1, keepdims=True)
    out_ref[...] = right / jnp.sqrt(d)


def basis_body(w_ref, keep_ref, got_ref, out_ref):
    core = lax.axis_index("core")
    for q, ref in ((core, keep_ref), (1 - core, got_ref)):
        w = w_ref[q][:, :72]
        out_ref[q] = dot(w, ref[...].astype(F32), precision=lax.Precision.HIGHEST)


def project_body(c_ref, w_ref, v_ref, out_ref):
    c = from_tiles(c_ref, 8).astype(BF)
    n = w_ref.shape[1]
    y = dot(c[:, :n], w_ref[...], 1, 1) + dot(c[:, n:], v_ref[...], 1, 1)
    peers = jnp.broadcast_to(y[None], (8, *y.shape))
    out_ref[...] = peers.reshape(out_ref.shape).astype(BF)


def final_body(w_ref, p_ref, out_ref):
    p = jnp.sum(p_ref[...].astype(F32), axis=0)
    out_ref[...] = dot(w_ref[...][:, :72], p, precision=lax.Precision.HIGHEST)


def on_device(acts, grads, basis_in, basis_out, eigen, sketch):
    lines = jnp.pad(acts.reshape(12, 1792), ((0, 4), (0, 0)))
    lines = lax.all_gather(lines, "core").reshape(32, 1792)
    packed = call(pack_body, ((64, 3584), BF), lines, limit=62)
    packed, own_grads, away_out = lax.optimization_barrier((packed, grads, basis_out))
    own_grads = own_grads.reshape(24, 256)
    own_grads, away_in = lax.optimization_barrier((own_grads, basis_in))
    far_out, far_in = from_sibling(away_out), from_sibling(away_in)
    near = swap(packed.reshape(8, 8, 3584), "z").reshape(64, 3584)
    near, own_grads, far_out, far_in = lax.optimization_barrier((near, own_grads, far_out, far_in))
    dense = call(dense_body, ((4, 48, 3584), BF), near, limit=62)
    all_grads = lax.all_gather(own_grads, ROW).reshape(384, 256)
    g_part = call(
        grad_body, ((2304, 128), BF), all_grads, sketch, basis_out, far_out, limit=62
    )
    both = swap(dense, "x").reshape(192, 3584)
    both, g_part, away = lax.optimization_barrier((both, g_part, eigen))
    g_pieces = swap(g_part.reshape(32, 9, 8, 128), COL)
    a_part = call(act_body, ((192, 896), BF), both, basis_in, far_in)
    a_part, g_pieces, far_eigen = lax.optimization_barrier((a_part, g_pieces, from_sibling(away)))
    g_own = call(sum_flat_body, ((2304, 128), BF), g_pieces, limit=62)
    a_own = summed(a_part.reshape(8, 24, 896), "y")
    a_own, g_own = lax.optimization_barrier((a_own, g_own))
    g_rot = swap(g_own.reshape(32, 9, 8, 128), COL)
    a_rot = lax.all_gather(a_own, ROW).reshape(8, 2, 24, 896)
    scaled, red = call(
        scaled_body, [((896, 1024), BF), ((8, 8, 8, 128), BF)],
        a_rot, g_rot, eigen, far_eigen,
    )
    reduced = sum_over(red, "y")
    span = call(range_body, ((32, 8, 8, 128), BF), reduced, basis_in, far_in)
    span = sum_over(span, COL)
    mapped, keep, give = call(
        mapped_body,
        [((8, 12, 8, 128), BF), ((72, 1792), BF), ((72, 1792), BF)],
        span, basis_in, far_in,
    )
    mapped = swap(call(gram_sum_body, ((8, 12, 8, 128), BF), swap(mapped, "y")), "y")
    core = call(core_body, ((768, 128), BF), mapped, scaled)
    core = swap(core.reshape(32, 3, 8, 128), COL)
    inverse = call(inverse_body, ((72, 128), F32), mapped)
    core, inverse, give = lax.optimization_barrier((core, inverse, give))
    core = call(sum_flat_body, ((768, 128), BF), core)
    core = swap(core.reshape(32, 3, 8, 128), COL)
    both_inverses = lax.all_gather(inverse, "core")
    core, both_inverses, got = lax.optimization_barrier((core, both_inverses, from_sibling(give)))
    part = call(project_body, ((576, 256), BF), core, basis_out, far_out)
    basis = call(basis_body, ((2, 72, 1792), F32), both_inverses, keep, got)
    mine = call(final_body, ((72, 256), F32), inverse, swap(part.reshape(8, 72, 256), "y"))
    return basis, lax.all_gather(mine, "core")


def solution(mesh):
    split = Mesh(mesh.devices.reshape(8, 2, 8, 4), ("y", "core", "z", "x"))
    return jax.shard_map(
        on_device,
        mesh=split,
        in_specs=(
            P(COL, None, ROW),
            P(ROW, None, COL),
            P(ROW, COL),
            P(COL, ROW),
            P(COL, ROW),
            P(None, COL),
        ),
        out_specs=(P(None, None, ROW), P(None, None, COL)),
        check_vma=False,
    )
```

```python
import jax
import jax.numpy as jnp
from jax import lax
from jax.experimental import pallas as pl
from jax.experimental.pallas import tpu as pltpu
from jax.sharding import Mesh
from jax.sharding import PartitionSpec as P

COL = ("z", "x")
ROW = ("y", "core")
BF = jnp.bfloat16
F32 = jnp.float32
MIB = 1024 * 1024


def call(body, out, *args, limit=52):
    many = isinstance(out, list)
    shapes = [jax.ShapeDtypeStruct(s, d) for s, d in (out if many else [out])]
    got = pl.pallas_call(
        body,
        out_shape=shapes,
        in_specs=[pl.BlockSpec(memory_space=pltpu.VMEM)] * len(args),
        out_specs=[pl.BlockSpec(memory_space=pltpu.VMEM)] * len(shapes),
        compiler_params=pltpu.CompilerParams(vmem_limit_bytes=limit * MIB),
    )(*args)
    return got if many else got[0]


def swap(x, axes):
    return lax.all_to_all(x, axes, 0, 0, tiled=True)


def from_sibling(x):
    return lax.ppermute(x, "core", [(0, 1), (1, 0)])


def dot(a, b, ca=1, cb=0, **kw):
    return lax.dot_general(a, b, (((ca,), (cb,)), ((), ())), preferred_element_type=F32, **kw)


def to_tiles(y, out_ref, slots=None):
    slots = slots or out_ref.shape[1]
    lanes = y.shape[1] // 128
    count = (y.shape[0] // 8) * lanes
    for t in range(out_ref.shape[0] * slots):
        if t < count:
            r, g = divmod(t, lanes)
            tile = y[r * 8 : r * 8 + 8, g * 128 : g * 128 + 128]
        else:
            tile = jnp.zeros((8, 128), F32)
        out_ref[t // slots, t % slots] = tile.astype(BF)


def to_flat_tiles(y, out_ref):
    lanes = y.shape[1] // 128
    count = (y.shape[0] // 8) * lanes

    def tile(t):
        r, g = divmod(t, lanes)
        return y[r * 8 : r * 8 + 8, g * 128 : g * 128 + 128] if t < count else jnp.zeros((8, 128), F32)

    for t in range(0, out_ref.shape[0] // 8, 2):
        pair = jnp.concatenate([tile(t), tile(t + 1)], axis=0)
        out_ref[t * 8 : t * 8 + 16] = pair.astype(BF)


def from_tiles(ref, lanes, rows=72, slots=None):
    slots = slots or ref.shape[1]
    lines = []
    for r in range(rows // 8):
        at = [divmod(r * lanes + g, slots) for g in range(lanes)]
        lines.append(jnp.concatenate([ref[p, s].astype(F32) for p, s in at], axis=1))
    return jnp.concatenate(lines, axis=0)


def sum_one_body(x_ref, out_ref):
    out_ref[...] = jnp.sum(x_ref[...].astype(F32), axis=0).astype(BF)


def summed(pieces, axes):
    own = swap(pieces, axes)
    return call(sum_one_body, (own.shape[1:], BF), own)


def sum_body(x_ref, out_ref):
    total = jnp.sum(x_ref[...].astype(F32), axis=0).astype(BF)
    out_ref[...] = jnp.broadcast_to(total[None], out_ref.shape)


def sum_flat_body(x_ref, out_ref):
    total = jnp.sum(x_ref[...].astype(F32), axis=0).reshape(-1, 128)
    peers = jnp.broadcast_to(total[None], (x_ref.shape[0], *total.shape))
    out_ref[...] = peers.reshape(out_ref.shape).astype(BF)


def sum_over(pieces, axes):
    own = swap(pieces, axes)
    return swap(call(sum_body, (own.shape, BF), own), axes)


def picked(n, to, x):
    rows = lax.broadcasted_iota(jnp.int32, (n, x.shape[0]), 0)
    return dot(jnp.where(rows == to, 1.0, 0.0).astype(BF), x).astype(BF)


def row_numbers(n):
    return lax.broadcasted_iota(jnp.int32, (1, n), 1)


def pack_body(x_ref, out_ref):
    core = lax.axis_index("core")
    m = row_numbers(32)
    token = (m & 15) >> 1
    parts = []
    for other in range(2):
        block = core if other == 0 else 1 - core
        mine = jnp.logical_and((m >> 4) == block, (m & 1) == core)
        parts.append(picked(8, jnp.where(mine, token, -1), x_ref[...]))
    packed = jnp.concatenate(parts, axis=1).astype(F32)
    peers = jnp.broadcast_to(packed[None], (8, *packed.shape))
    out_ref[...] = peers.reshape(out_ref.shape).astype(BF)


def dense_body(x_ref, out_ref):
    m = row_numbers(64)
    token = m & 7
    y = picked(48, jnp.where(token < 6, (m >> 3) * 6 + token, -1), x_ref[...])
    out_ref[...] = jnp.broadcast_to(y[None], out_ref.shape)


def act_body(x_ref, w_ref, v_ref, out_ref):
    n = w_ref.shape[0]
    y = dot(x_ref[:, :n], w_ref[...]) + dot(x_ref[:, n:], v_ref[...])
    out_ref[...] = y.astype(BF)


def grad_body(g_ref, s_ref, w_ref, v_ref, out_ref):
    m = row_numbers(384)
    token = m >> 1
    peer = jnp.floor((token.astype(F32) + 0.5) * (1.0 / 6.0)).astype(jnp.int32)
    to = (peer & 3) * 48 + (peer >> 2) * 6 + token - peer * 6
    g = picked(192, jnp.where((m & 1) == lax.axis_index("core"), to, -1), g_ref[...])
    s = s_ref[...]
    w, v = w_ref[...], v_ref[...]
    top = jnp.concatenate([dot(g, w), dot(g, v)], axis=1)
    low = jnp.concatenate([dot(s, w), dot(s, v)], axis=1)
    to_flat_tiles(jnp.concatenate([top, low], axis=0), out_ref)


def scaled_body(a_ref, g_ref, e_ref, f_ref, scaled_ref, out_ref):
    core = lax.axis_index("core")
    a = jnp.concatenate([a_ref[y, core].astype(F32) for y in range(8)], axis=0).astype(BF)
    g = from_tiles(g_ref, 8, 264)
    both = dot(a.T, g[:192].astype(BF))
    n = e_ref.shape[1]
    left = (both[:, :n] / e_ref[...].astype(F32)).astype(BF)
    right = (both[:, n:] / f_ref[...].astype(F32)).astype(BF)
    s = jnp.concatenate([left, right], axis=1)
    scaled_ref[...] = s
    to_tiles(dot(g[192:].astype(BF), s, 1, 1), out_ref)


def range_body(r_ref, w_ref, v_ref, out_ref):
    r = from_tiles(r_ref, 7).astype(BF)
    both = [dot(r, w_ref[...], 1, 1), dot(r, v_ref[...], 1, 1)]
    to_tiles(jnp.concatenate(both, axis=1), out_ref)


def split3(x):
    hi = x.astype(BF)
    left = x - hi.astype(F32)
    mid = left.astype(BF)
    return hi, mid, (left - mid.astype(F32)).astype(BF)


def gram_at(g):
    return (g, 9) if g < 8 else (7, 6)


def mapped_body(r_ref, w_ref, v_ref, out_ref, keep_ref, give_ref):
    r = from_tiles(r_ref, 28).astype(BF)
    n = w_ref.shape[0]
    keep_ref[...] = r[:, :n]
    give_ref[...] = r[:, n:]
    to_tiles(dot(r[:, :n], w_ref[...]) + dot(r[:, n:], v_ref[...]), out_ref, 9)
    gram = jnp.concatenate([dot(r, r, 1, 1), jnp.zeros((72, 56), F32)], axis=1)
    for g in range(9):
        p, s = gram_at(g)
        for i, part in enumerate(split3(gram[g * 8 : g * 8 + 8])):
            out_ref[p, s + i] = part


def gram_sum_body(x_ref, out_ref):
    total = jnp.sum(x_ref[...].astype(F32), axis=0)
    last = lax.axis_index("y") == 7
    parts = split3(total[9] + total[10] + total[11])
    spare = split3(total[6] + total[7] + total[8])
    for i in range(12):
        tile = total[i].astype(BF)
        if i >= 9:
            tile = parts[i - 9]
        elif i >= 6:
            tile = jnp.where(last, spare[i - 6].astype(F32), total[i]).astype(BF)
        out_ref[:, i] = jnp.broadcast_to(tile[None], (out_ref.shape[0], 8, 128))


def core_body(m_ref, s_ref, out_ref):
    m = from_tiles(m_ref, 7, slots=9).astype(BF)
    to_flat_tiles(dot(m, s_ref[...]), out_ref)


def inverse_body(m_ref, out_ref):
    tiles = []
    for g in range(9):
        p, s = gram_at(g)
        tiles.append(sum(m_ref[p, s + i].astype(F32) for i in range(3)))
    left = jnp.concatenate(tiles, axis=0)
    rows = lax.broadcasted_iota(jnp.int32, (72, 128), 0)
    lanes = lax.broadcasted_iota(jnp.int32, (72, 128), 1)
    below = lax.broadcasted_iota(jnp.int32, (72, 1), 0)
    right = jnp.where(rows == lanes, 1.0, 0.0)
    for k in range(72):
        pivot = left[k : k + 1]
        f = left[:, k : k + 1] / pivot[:, k : k + 1]
        f = jnp.where(below > k, f, 0.0)
        line = right[k : k + 1]
        left = left - f * pivot
        right = right - f * line
    d = jnp.sum(jnp.where(rows == lanes, left, 0.0), axis=1, keepdims=True)
    out_ref[...] = right / jnp.sqrt(d)


def basis_body(w_ref, keep_ref, got_ref, out_ref):
    core = lax.axis_index("core")
    for q, ref in ((core, keep_ref), (1 - core, got_ref)):
        w = w_ref[q][:, :72]
        out_ref[q] = dot(w, ref[...].astype(F32), precision=lax.Precision.HIGHEST)


def project_body(c_ref, w_ref, v_ref, out_ref):
    c = from_tiles(c_ref, 8).astype(BF)
    n = w_ref.shape[1]
    y = dot(c[:, :n], w_ref[...], 1, 1) + dot(c[:, n:], v_ref[...], 1, 1)
    peers = jnp.broadcast_to(y[None], (8, *y.shape))
    out_ref[...] = peers.reshape(out_ref.shape).astype(BF)


def final_body(w_ref, p_ref, out_ref):
    p = jnp.sum(p_ref[...].astype(F32), axis=0)
    out_ref[...] = dot(w_ref[...][:, :72], p, precision=lax.Precision.HIGHEST)


def on_device(acts, grads, basis_in, basis_out, eigen, sketch):
    lines = jnp.pad(acts.reshape(12, 1792), ((0, 4), (0, 0)))
    lines = lax.all_gather(lines, "core").reshape(32, 1792)
    packed = call(pack_body, ((64, 3584), BF), lines)
    packed, own_grads = lax.optimization_barrier((packed, grads))
    all_grads = lax.all_gather(own_grads.reshape(24, 256), ROW).reshape(384, 256)
    near = swap(packed.reshape(8, 8, 3584), "z").reshape(64, 3584)
    near, all_grads, away = lax.optimization_barrier(
        (near, all_grads, (basis_in, basis_out, eigen))
    )
    dense = call(dense_body, ((4, 48, 3584), BF), near)
    far_in, far_out, far_eigen = [from_sibling(w) for w in away]
    g_part = call(
        grad_body, ((2304, 128), BF), all_grads, sketch, basis_out, far_out
    )
    both = swap(dense, "x").reshape(192, 3584)
    both, g_part, far_in, far_eigen = lax.optimization_barrier((both, g_part, far_in, far_eigen))
    g_pieces = swap(g_part.reshape(32, 9, 8, 128), COL)
    a_part = call(act_body, ((192, 896), BF), both, basis_in, far_in)
    a_part, g_pieces = lax.optimization_barrier((a_part, g_pieces))
    g_own = call(sum_flat_body, ((2304, 128), BF), g_pieces)
    a_own = summed(a_part.reshape(8, 24, 896), "y")
    a_own, g_own = lax.optimization_barrier((a_own, g_own))
    g_rot = swap(g_own.reshape(32, 9, 8, 128), COL)
    a_rot = lax.all_gather(a_own, ROW).reshape(8, 2, 24, 896)
    scaled, red = call(
        scaled_body, [((896, 1024), BF), ((8, 8, 8, 128), BF)],
        a_rot, g_rot, eigen, far_eigen,
    )
    reduced = sum_over(red, "y")
    span = call(range_body, ((32, 8, 8, 128), BF), reduced, basis_in, far_in)
    span = sum_over(span, COL)
    mapped, keep, give = call(
        mapped_body,
        [((8, 12, 8, 128), BF), ((72, 1792), BF), ((72, 1792), BF)],
        span, basis_in, far_in,
    )
    mapped = swap(call(gram_sum_body, ((8, 12, 8, 128), BF), swap(mapped, "y")), "y")
    core = call(core_body, ((768, 128), BF), mapped, scaled)
    core = swap(core.reshape(32, 3, 8, 128), COL)
    inverse = call(inverse_body, ((72, 128), F32), mapped)
    core, inverse, give = lax.optimization_barrier((core, inverse, give))
    core = call(sum_flat_body, ((768, 128), BF), core)
    core = swap(core.reshape(32, 3, 8, 128), COL)
    both_inverses = lax.all_gather(inverse, "core")
    core, both_inverses, got = lax.optimization_barrier((core, both_inverses, from_sibling(give)))
    part = call(project_body, ((576, 256), BF), core, basis_out, far_out)
    basis = call(basis_body, ((2, 72, 1792), F32), both_inverses, keep, got)
    mine = call(final_body, ((72, 256), F32), inverse, swap(part.reshape(8, 72, 256), "y"))
    return basis, lax.all_gather(mine, "core")


def solution(mesh):
    split = Mesh(mesh.devices.reshape(8, 2, 8, 4), ("y", "core", "z", "x"))
    return jax.shard_map(
        on_device,
        mesh=split,
        in_specs=(
            P(COL, None, ROW),
            P(ROW, None, COL),
            P(ROW, COL),
            P(COL, ROW),
            P(COL, ROW),
            P(None, COL),
        ),
        out_specs=(P(None, None, ROW), P(None, None, COL)),
        check_vma=False,
    )
```

```python
import jax
import jax.numpy as jnp
from jax import lax
from jax.experimental import pallas as pl
from jax.experimental.pallas import tpu as pltpu
from jax.sharding import Mesh
from jax.sharding import PartitionSpec as P

COL = ("z", "x")
ROW = ("y", "core")
BF = jnp.bfloat16
F32 = jnp.float32
MIB = 1024 * 1024


class Late:
    def __init__(self, source, buffer, semaphore):
        self.copy = pltpu.make_async_copy(source, buffer, semaphore)
        self.copy.start()
        self.buffer, self.shape = buffer, buffer.shape

    def get(self):
        self.copy.wait()
        return self.buffer[...]


def call(body, out, *args, late=(), limit=32):
    many = isinstance(out, list)
    shapes = [jax.ShapeDtypeStruct(s, d) for s, d in (out if many else [out])]
    n, m = len(args), len(shapes)
    whole, away = pl.BlockSpec(memory_space=pltpu.VMEM), pl.BlockSpec(memory_space=pltpu.HBM)
    buffers = [pltpu.VMEM(args[i].shape, args[i].dtype) for i in late]

    def run(*refs):
        given, held = list(refs[:n]), refs[n + m :]
        for k, i in enumerate(late):
            given[i] = Late(given[i], held[k], held[-1].at[k])
        body(*given, *refs[n : n + m])

    got = pl.pallas_call(
        run if late else body,
        out_shape=shapes,
        in_specs=[away if i in late else whole for i in range(n)],
        out_specs=[whole] * m,
        scratch_shapes=buffers + [pltpu.SemaphoreType.DMA((len(late),))] if late else (),
        compiler_params=pltpu.CompilerParams(vmem_limit_bytes=limit * MIB),
    )(*args)
    return got if many else got[0]


def swap(x, axes):
    return lax.all_to_all(x, axes, 0, 0, tiled=True)


def from_sibling(x):
    return lax.ppermute(x, "core", [(0, 1), (1, 0)])


def dot(a, b, ca=1, cb=0, **kw):
    return lax.dot_general(a, b, (((ca,), (cb,)), ((), ())), preferred_element_type=F32, **kw)


def to_tiles(y, out_ref, slots=None):
    slots = slots or out_ref.shape[1]
    lanes = y.shape[1] // 128
    count = (y.shape[0] // 8) * lanes
    for t in range(out_ref.shape[0] * slots):
        if t < count:
            r, g = divmod(t, lanes)
            tile = y[r * 8 : r * 8 + 8, g * 128 : g * 128 + 128]
        else:
            tile = jnp.zeros((8, 128), F32)
        out_ref[t // slots, t % slots] = tile.astype(BF)


def to_flat_tiles(y, out_ref):
    lanes = y.shape[1] // 128
    count = (y.shape[0] // 8) * lanes

    def tile(t):
        r, g = divmod(t, lanes)
        return y[r * 8 : r * 8 + 8, g * 128 : g * 128 + 128] if t < count else jnp.zeros((8, 128), F32)

    for t in range(0, out_ref.shape[0] // 8, 2):
        pair = jnp.concatenate([tile(t), tile(t + 1)], axis=0)
        out_ref[t * 8 : t * 8 + 16] = pair.astype(BF)


def from_tiles(ref, lanes, rows=72, slots=None):
    slots = slots or ref.shape[1]
    lines = []
    for r in range(rows // 8):
        at = [divmod(r * lanes + g, slots) for g in range(lanes)]
        lines.append(jnp.concatenate([ref[p, s].astype(F32) for p, s in at], axis=1))
    return jnp.concatenate(lines, axis=0)


def sum_one_body(x_ref, out_ref):
    out_ref[...] = jnp.sum(x_ref[...].astype(F32), axis=0).astype(BF)


def summed(pieces, axes):
    own = swap(pieces, axes)
    return call(sum_one_body, (own.shape[1:], BF), own)


def sum_body(x_ref, out_ref):
    total = jnp.sum(x_ref[...].astype(F32), axis=0).astype(BF)
    out_ref[...] = jnp.broadcast_to(total[None], out_ref.shape)


def sum_flat_body(x_ref, out_ref):
    total = jnp.sum(x_ref[...].astype(F32), axis=0).reshape(-1, 128)
    peers = jnp.broadcast_to(total[None], (x_ref.shape[0], *total.shape))
    out_ref[...] = peers.reshape(out_ref.shape).astype(BF)


def sum_over(pieces, axes):
    own = swap(pieces, axes)
    return swap(call(sum_body, (own.shape, BF), own), axes)


def picked(n, to, x):
    rows = lax.broadcasted_iota(jnp.int32, (n, x.shape[0]), 0)
    return dot(jnp.where(rows == to, 1.0, 0.0).astype(BF), x).astype(BF)


def row_numbers(n):
    return lax.broadcasted_iota(jnp.int32, (1, n), 1)


def pack_body(x_ref, out_ref):
    core = lax.axis_index("core")
    m = row_numbers(32)
    token = (m & 15) >> 1
    parts = []
    for other in range(2):
        block = core if other == 0 else 1 - core
        mine = jnp.logical_and((m >> 4) == block, (m & 1) == core)
        parts.append(picked(8, jnp.where(mine, token, -1), x_ref[...]))
    packed = jnp.concatenate(parts, axis=1).astype(F32)
    peers = jnp.broadcast_to(packed[None], (8, *packed.shape))
    out_ref[...] = peers.reshape(out_ref.shape).astype(BF)


def dense_body(x_ref, out_ref):
    m = row_numbers(64)
    token = m & 7
    y = picked(48, jnp.where(token < 6, (m >> 3) * 6 + token, -1), x_ref[...])
    out_ref[...] = jnp.broadcast_to(y[None], out_ref.shape)


def act_body(x_ref, w_ref, v_ref, out_ref):
    n = w_ref.shape[0]
    y = dot(x_ref[:, :n], w_ref[...]) + dot(x_ref[:, n:], v_ref[...])
    out_ref[...] = y.astype(BF)


def grad_body(g_ref, s_ref, w_ref, v_ref, out_ref):
    m = row_numbers(384)
    token = m >> 1
    peer = jnp.floor((token.astype(F32) + 0.5) * (1.0 / 6.0)).astype(jnp.int32)
    to = (peer & 3) * 48 + (peer >> 2) * 6 + token - peer * 6
    g = picked(192, jnp.where((m & 1) == lax.axis_index("core"), to, -1), g_ref[...])
    s = s_ref[...]
    w, v = w_ref[...], v_ref[...]
    top = jnp.concatenate([dot(g, w), dot(g, v)], axis=1)
    low = jnp.concatenate([dot(s, w), dot(s, v)], axis=1)
    to_flat_tiles(jnp.concatenate([top, low], axis=0), out_ref)


def scaled_body(a_ref, g_ref, e_ref, f_ref, scaled_ref, out_ref):
    core = lax.axis_index("core")
    a = jnp.concatenate([a_ref[y, core].astype(F32) for y in range(8)], axis=0).astype(BF)
    g = from_tiles(g_ref, 8, 264)
    both = dot(a.T, g[:192].astype(BF))
    n = e_ref.shape[1]
    left = (both[:, :n] / e_ref[...].astype(F32)).astype(BF)
    right = (both[:, n:] / f_ref[...].astype(F32)).astype(BF)
    s = jnp.concatenate([left, right], axis=1)
    scaled_ref[...] = s
    to_tiles(dot(g[192:].astype(BF), s, 1, 1), out_ref)


def range_body(r_ref, w_ref, v_ref, out_ref):
    r = from_tiles(r_ref, 7).astype(BF)
    both = [dot(r, w_ref[...], 1, 1), dot(r, v_ref.get(), 1, 1)]
    to_tiles(jnp.concatenate(both, axis=1), out_ref)


def split3(x):
    hi = x.astype(BF)
    left = x - hi.astype(F32)
    mid = left.astype(BF)
    return hi, mid, (left - mid.astype(F32)).astype(BF)


def gram_at(g):
    return (g, 9) if g < 8 else (7, 6)


def mapped_body(r_ref, w_ref, v_ref, out_ref, keep_ref, give_ref):
    r = from_tiles(r_ref, 28).astype(BF)
    n = w_ref.shape[0]
    keep_ref[...] = r[:, :n]
    give_ref[...] = r[:, n:]
    to_tiles(dot(r[:, :n], w_ref[...]) + dot(r[:, n:], v_ref.get()), out_ref, 9)
    gram = jnp.concatenate([dot(r, r, 1, 1), jnp.zeros((72, 56), F32)], axis=1)
    for g in range(9):
        p, s = gram_at(g)
        for i, part in enumerate(split3(gram[g * 8 : g * 8 + 8])):
            out_ref[p, s + i] = part


def gram_sum_body(x_ref, out_ref):
    total = jnp.sum(x_ref[...].astype(F32), axis=0)
    last = lax.axis_index("y") == 7
    parts = split3(total[9] + total[10] + total[11])
    spare = split3(total[6] + total[7] + total[8])
    for i in range(12):
        tile = total[i].astype(BF)
        if i >= 9:
            tile = parts[i - 9]
        elif i >= 6:
            tile = jnp.where(last, spare[i - 6].astype(F32), total[i]).astype(BF)
        out_ref[:, i] = jnp.broadcast_to(tile[None], (out_ref.shape[0], 8, 128))


def core_body(m_ref, s_ref, out_ref):
    m = from_tiles(m_ref, 7, slots=9).astype(BF)
    to_flat_tiles(dot(m, s_ref[...]), out_ref)


def inverse_body(m_ref, out_ref):
    tiles = []
    for g in range(9):
        p, s = gram_at(g)
        tiles.append(sum(m_ref[p, s + i].astype(F32) for i in range(3)))
    left = jnp.concatenate(tiles, axis=0)
    rows = lax.broadcasted_iota(jnp.int32, (72, 128), 0)
    lanes = lax.broadcasted_iota(jnp.int32, (72, 128), 1)
    below = lax.broadcasted_iota(jnp.int32, (72, 1), 0)
    right = jnp.where(rows == lanes, 1.0, 0.0)
    for k in range(72):
        pivot = left[k : k + 1]
        f = left[:, k : k + 1] / pivot[:, k : k + 1]
        f = jnp.where(below > k, f, 0.0)
        line = right[k : k + 1]
        left = left - f * pivot
        right = right - f * line
    d = jnp.sum(jnp.where(rows == lanes, left, 0.0), axis=1, keepdims=True)
    out_ref[...] = right / jnp.sqrt(d)


def basis_body(w_ref, keep_ref, got_ref, out_ref):
    core = lax.axis_index("core")
    for q, ref in ((core, keep_ref), (1 - core, got_ref)):
        w = w_ref[q][:, :72]
        out_ref[q] = dot(w, ref[...].astype(F32), precision=lax.Precision.HIGHEST)


def project_body(c_ref, w_ref, v_ref, out_ref):
    c = from_tiles(c_ref, 8).astype(BF)
    n = w_ref.shape[1]
    y = dot(c[:, :n], w_ref[...], 1, 1) + dot(c[:, n:], v_ref[...], 1, 1)
    peers = jnp.broadcast_to(y[None], (8, *y.shape))
    out_ref[...] = peers.reshape(out_ref.shape).astype(BF)


def final_body(w_ref, p_ref, out_ref):
    p = jnp.sum(p_ref[...].astype(F32), axis=0)
    out_ref[...] = dot(w_ref[...][:, :72], p, precision=lax.Precision.HIGHEST)


def on_device(acts, grads, basis_in, basis_out, eigen, sketch):
    lines = jnp.pad(acts.reshape(12, 1792), ((0, 4), (0, 0)))
    lines = lax.all_gather(lines, "core").reshape(32, 1792)
    packed = call(pack_body, ((64, 3584), BF), lines, limit=62)
    packed, own_grads = lax.optimization_barrier((packed, grads))
    all_grads = lax.all_gather(own_grads.reshape(24, 256), ROW).reshape(384, 256)
    near = swap(packed.reshape(8, 8, 3584), "z").reshape(64, 3584)
    near, all_grads, away = lax.optimization_barrier(
        (near, all_grads, (basis_in, basis_out, eigen))
    )
    dense = call(dense_body, ((4, 48, 3584), BF), near, limit=62)
    far_in, far_out, far_eigen = [from_sibling(w) for w in away]
    g_part = call(
        grad_body, ((2304, 128), BF), all_grads, sketch, basis_out, far_out, limit=62
    )
    both = swap(dense, "x").reshape(192, 3584)
    both, g_part, far_in, far_eigen = lax.optimization_barrier((both, g_part, far_in, far_eigen))
    g_pieces = swap(g_part.reshape(32, 9, 8, 128), COL)
    a_part = call(act_body, ((192, 896), BF), both, basis_in, far_in)
    a_part, g_pieces = lax.optimization_barrier((a_part, g_pieces))
    g_own = call(sum_flat_body, ((2304, 128), BF), g_pieces)
    a_own = summed(a_part.reshape(8, 24, 896), "y")
    a_own, g_own = lax.optimization_barrier((a_own, g_own))
    g_rot = swap(g_own.reshape(32, 9, 8, 128), COL)
    a_rot = lax.all_gather(a_own, ROW).reshape(8, 2, 24, 896)
    scaled, red = call(
        scaled_body, [((896, 1024), BF), ((8, 8, 8, 128), BF)],
        a_rot, g_rot, eigen, far_eigen,
    )
    reduced = sum_over(red, "y")
    span = call(range_body, ((32, 8, 8, 128), BF), reduced, basis_in, far_in, late=(2,))
    span = sum_over(span, COL)
    mapped, keep, give = call(
        mapped_body,
        [((8, 12, 8, 128), BF), ((72, 1792), BF), ((72, 1792), BF)],
        span, basis_in, far_in, late=(2,),
    )
    mapped = swap(call(gram_sum_body, ((8, 12, 8, 128), BF), swap(mapped, "y")), "y")
    core = call(core_body, ((768, 128), BF), mapped, scaled)
    core = swap(core.reshape(32, 3, 8, 128), COL)
    inverse = call(inverse_body, ((72, 128), F32), mapped)
    core, inverse, got = lax.optimization_barrier((core, inverse, from_sibling(give)))
    core = swap(call(sum_flat_body, ((768, 128), BF), core).reshape(32, 3, 8, 128), COL)
    core, given = lax.optimization_barrier((core, inverse))
    both_inverses = lax.all_gather(given, "core")
    part = call(project_body, ((576, 256), BF), core, basis_out, far_out)
    basis = call(basis_body, ((2, 72, 1792), F32), both_inverses, keep, got)
    mine = call(final_body, ((72, 256), F32), inverse, swap(part.reshape(8, 72, 256), "y"))
    return basis, lax.all_gather(mine, "core")


def solution(mesh):
    split = Mesh(mesh.devices.reshape(8, 2, 8, 4), ("y", "core", "z", "x"))
    return jax.shard_map(
        on_device,
        mesh=split,
        in_specs=(
            P(COL, None, ROW),
            P(ROW, None, COL),
            P(ROW, COL),
            P(COL, ROW),
            P(COL, ROW),
            P(None, COL),
        ),
        out_specs=(P(None, None, ROW), P(None, None, COL)),
        check_vma=False,
    )
```

```python
import jax
import jax.numpy as jnp
from jax import lax
from jax.experimental import pallas as pl
from jax.experimental.pallas import tpu as pltpu
from jax.sharding import Mesh
from jax.sharding import PartitionSpec as P

COL = ("z", "x")
ROW = ("y", "core")
BF = jnp.bfloat16
F32 = jnp.float32
MIB = 1024 * 1024
FRONT = 60


def call(body, out, *args, limit=32):
    many = isinstance(out, list)
    shapes = [jax.ShapeDtypeStruct(s, d) for s, d in (out if many else [out])]
    got = pl.pallas_call(
        body,
        out_shape=shapes,
        in_specs=[pl.BlockSpec(memory_space=pltpu.VMEM)] * len(args),
        out_specs=[pl.BlockSpec(memory_space=pltpu.VMEM)] * len(shapes),
        compiler_params=pltpu.CompilerParams(vmem_limit_bytes=limit * MIB),
    )(*args)
    return got if many else got[0]


def swap(x, axes):
    return lax.all_to_all(x, axes, 0, 0, tiled=True)


def from_sibling(x):
    return lax.ppermute(x, "core", [(0, 1), (1, 0)])


def dot(a, b, ca=1, cb=0, **kw):
    return lax.dot_general(a, b, (((ca,), (cb,)), ((), ())), preferred_element_type=F32, **kw)


def to_tiles(y, out_ref, slots=None):
    slots = slots or out_ref.shape[1]
    lanes = y.shape[1] // 128
    count = (y.shape[0] // 8) * lanes
    for t in range(out_ref.shape[0] * slots):
        if t < count:
            r, g = divmod(t, lanes)
            tile = y[r * 8 : r * 8 + 8, g * 128 : g * 128 + 128]
        else:
            tile = jnp.zeros((8, 128), F32)
        out_ref[t // slots, t % slots] = tile.astype(BF)


def to_flat_tiles(y, out_ref):
    lanes = y.shape[1] // 128
    count = (y.shape[0] // 8) * lanes

    def tile(t):
        r, g = divmod(t, lanes)
        return y[r * 8 : r * 8 + 8, g * 128 : g * 128 + 128] if t < count else jnp.zeros((8, 128), F32)

    for t in range(0, out_ref.shape[0] // 8, 2):
        pair = jnp.concatenate([tile(t), tile(t + 1)], axis=0)
        out_ref[t * 8 : t * 8 + 16] = pair.astype(BF)


def from_tiles(ref, lanes, rows=72, slots=None):
    slots = slots or ref.shape[1]
    lines = []
    for r in range(rows // 8):
        at = [divmod(r * lanes + g, slots) for g in range(lanes)]
        lines.append(jnp.concatenate([ref[p, s].astype(F32) for p, s in at], axis=1))
    return jnp.concatenate(lines, axis=0)


def sum_one_body(x_ref, out_ref):
    out_ref[...] = jnp.sum(x_ref[...].astype(F32), axis=0).astype(BF)


def summed(pieces, axes):
    own = swap(pieces, axes)
    return call(sum_one_body, (own.shape[1:], BF), own)


def sum_body(x_ref, out_ref):
    total = jnp.sum(x_ref[...].astype(F32), axis=0).astype(BF)
    out_ref[...] = jnp.broadcast_to(total[None], out_ref.shape)


def sum_flat_body(x_ref, out_ref):
    total = jnp.sum(x_ref[...].astype(F32), axis=0).reshape(-1, 128)
    peers = jnp.broadcast_to(total[None], (x_ref.shape[0], *total.shape))
    out_ref[...] = peers.reshape(out_ref.shape).astype(BF)


def sum_over(pieces, axes):
    own = swap(pieces, axes)
    return swap(call(sum_body, (own.shape, BF), own), axes)


def picked(n, to, x):
    rows = lax.broadcasted_iota(jnp.int32, (n, x.shape[0]), 0)
    return dot(jnp.where(rows == to, 1.0, 0.0).astype(BF), x).astype(BF)


def row_numbers(n):
    return lax.broadcasted_iota(jnp.int32, (1, n), 1)


def pack_body(x_ref, out_ref):
    core = lax.axis_index("core")
    m = row_numbers(32)
    token = (m & 15) >> 1
    parts = []
    for other in range(2):
        block = core if other == 0 else 1 - core
        mine = jnp.logical_and((m >> 4) == block, (m & 1) == core)
        parts.append(picked(8, jnp.where(mine, token, -1), x_ref[...]))
    packed = jnp.concatenate(parts, axis=1).astype(F32)
    peers = jnp.broadcast_to(packed[None], (8, *packed.shape))
    out_ref[...] = peers.reshape(out_ref.shape).astype(BF)


def dense_body(x_ref, out_ref):
    m = row_numbers(64)
    token = m & 7
    y = picked(48, jnp.where(token < 6, (m >> 3) * 6 + token, -1), x_ref[...])
    out_ref[...] = jnp.broadcast_to(y[None], out_ref.shape)


def act_body(x_ref, w_ref, v_ref, out_ref):
    n = w_ref.shape[0]
    y = dot(x_ref[:, :n], w_ref[...]) + dot(x_ref[:, n:], v_ref[...])
    out_ref[...] = y.astype(BF)


def grad_body(g_ref, s_ref, w_ref, v_ref, out_ref):
    m = row_numbers(384)
    token = m >> 1
    peer = jnp.floor((token.astype(F32) + 0.5) * (1.0 / 6.0)).astype(jnp.int32)
    to = (peer & 3) * 48 + (peer >> 2) * 6 + token - peer * 6
    g = picked(192, jnp.where((m & 1) == lax.axis_index("core"), to, -1), g_ref[...])
    s = s_ref[...]
    w, v = w_ref[...], v_ref[...]
    top = jnp.concatenate([dot(g, w), dot(g, v)], axis=1)
    low = jnp.concatenate([dot(s, w), dot(s, v)], axis=1)
    to_flat_tiles(jnp.concatenate([top, low], axis=0), out_ref)


def scaled_body(a_ref, g_ref, e_ref, f_ref, scaled_ref, out_ref):
    core = lax.axis_index("core")
    a = jnp.concatenate([a_ref[y, core].astype(F32) for y in range(8)], axis=0).astype(BF)
    g = from_tiles(g_ref, 8, 264)
    both = dot(a.T, g[:192].astype(BF))
    n = e_ref.shape[1]
    left = (both[:, :n] / e_ref[...].astype(F32)).astype(BF)
    right = (both[:, n:] / f_ref[...].astype(F32)).astype(BF)
    s = jnp.concatenate([left, right], axis=1)
    scaled_ref[...] = s
    to_tiles(dot(g[192:].astype(BF), s, 1, 1), out_ref)


def range_body(r_ref, w_ref, v_ref, out_ref):
    r = from_tiles(r_ref, 7).astype(BF)
    both = [dot(r, w_ref[...], 1, 1), dot(r, v_ref[...], 1, 1)]
    to_tiles(jnp.concatenate(both, axis=1), out_ref)


def split3(x):
    hi = x.astype(BF)
    left = x - hi.astype(F32)
    mid = left.astype(BF)
    return hi, mid, (left - mid.astype(F32)).astype(BF)


def gram_at(g):
    return (g, 9) if g < 8 else (7, 6)


def mapped_body(r_ref, w_ref, v_ref, out_ref, keep_ref, give_ref):
    r = from_tiles(r_ref, 28).astype(BF)
    n = w_ref.shape[0]
    keep_ref[...] = r[:, :n]
    give_ref[...] = r[:, n:]
    to_tiles(dot(r[:, :n], w_ref[...]) + dot(r[:, n:], v_ref[...]), out_ref, 9)
    gram = jnp.concatenate([dot(r, r, 1, 1), jnp.zeros((72, 56), F32)], axis=1)
    for g in range(9):
        p, s = gram_at(g)
        for i, part in enumerate(split3(gram[g * 8 : g * 8 + 8])):
            out_ref[p, s + i] = part


def gram_sum_body(x_ref, out_ref):
    total = jnp.sum(x_ref[...].astype(F32), axis=0)
    last = lax.axis_index("y") == 7
    parts = split3(total[9] + total[10] + total[11])
    spare = split3(total[6] + total[7] + total[8])
    for i in range(12):
        tile = total[i].astype(BF)
        if i >= 9:
            tile = parts[i - 9]
        elif i >= 6:
            tile = jnp.where(last, spare[i - 6].astype(F32), total[i]).astype(BF)
        out_ref[:, i] = jnp.broadcast_to(tile[None], (out_ref.shape[0], 8, 128))


def core_body(m_ref, s_ref, out_ref):
    m = from_tiles(m_ref, 7, slots=9).astype(BF)
    to_flat_tiles(dot(m, s_ref[...]), out_ref)


def inverse_body(m_ref, out_ref):
    tiles = []
    for g in range(9):
        p, s = gram_at(g)
        tiles.append(sum(m_ref[p, s + i].astype(F32) for i in range(3)))
    left = jnp.concatenate(tiles, axis=0)
    rows = lax.broadcasted_iota(jnp.int32, (72, 128), 0)
    lanes = lax.broadcasted_iota(jnp.int32, (72, 128), 1)
    below = lax.broadcasted_iota(jnp.int32, (72, 1), 0)
    right = jnp.where(rows == lanes, 1.0, 0.0)
    for k in range(72):
        pivot = left[k : k + 1]
        f = left[:, k : k + 1] / pivot[:, k : k + 1]
        f = jnp.where(below > k, f, 0.0)
        line = right[k : k + 1]
        left = left - f * pivot
        right = right - f * line
    d = jnp.sum(jnp.where(rows == lanes, left, 0.0), axis=1, keepdims=True)
    out_ref[...] = right / jnp.sqrt(d)


def basis_body(w_ref, keep_ref, got_ref, out_ref):
    core = lax.axis_index("core")
    for q, ref in ((core, keep_ref), (1 - core, got_ref)):
        w = w_ref[q][:, :72]
        out_ref[q] = dot(w, ref[...].astype(F32), precision=lax.Precision.HIGHEST)


def project_body(c_ref, w_ref, v_ref, out_ref):
    c = from_tiles(c_ref, 8).astype(BF)
    n = w_ref.shape[1]
    y = dot(c[:, :n], w_ref[...], 1, 1) + dot(c[:, n:], v_ref[...], 1, 1)
    peers = jnp.broadcast_to(y[None], (8, *y.shape))
    out_ref[...] = peers.reshape(out_ref.shape).astype(BF)


def final_body(w_ref, p_ref, out_ref):
    p = jnp.sum(p_ref[...].astype(F32), axis=0)
    out_ref[...] = dot(w_ref[...][:, :72], p, precision=lax.Precision.HIGHEST)


def on_device(acts, grads, basis_in, basis_out, eigen, sketch):
    lines = jnp.pad(acts.reshape(12, 1792), ((0, 4), (0, 0)))
    lines = lax.all_gather(lines, "core").reshape(32, 1792)
    packed = call(pack_body, ((64, 3584), BF), lines, limit=FRONT)
    packed, own_grads = lax.optimization_barrier((packed, grads))
    all_grads = lax.all_gather(own_grads.reshape(24, 256), ROW).reshape(384, 256)
    near = swap(packed.reshape(8, 8, 3584), "z").reshape(64, 3584)
    near, all_grads, away = lax.optimization_barrier(
        (near, all_grads, (basis_in, basis_out, eigen))
    )
    dense = call(dense_body, ((4, 48, 3584), BF), near, limit=FRONT)
    far_in, far_out, far_eigen = [from_sibling(w) for w in away]
    g_part = call(
        grad_body, ((2304, 128), BF), all_grads, sketch, basis_out, far_out, limit=FRONT
    )
    both = swap(dense, "x").reshape(192, 3584)
    both, g_part, far_in, far_eigen = lax.optimization_barrier((both, g_part, far_in, far_eigen))
    g_pieces = swap(g_part.reshape(32, 9, 8, 128), COL)
    a_part = call(act_body, ((192, 896), BF), both, basis_in, far_in, limit=FRONT)
    a_part, g_pieces = lax.optimization_barrier((a_part, g_pieces))
    g_own = call(sum_flat_body, ((2304, 128), BF), g_pieces, limit=FRONT)
    a_own = summed(a_part.reshape(8, 24, 896), "y")
    a_own, g_own = lax.optimization_barrier((a_own, g_own))
    g_rot = swap(g_own.reshape(32, 9, 8, 128), COL)
    a_rot = lax.all_gather(a_own, ROW).reshape(8, 2, 24, 896)
    scaled, red = call(
        scaled_body, [((896, 1024), BF), ((8, 8, 8, 128), BF)],
        a_rot, g_rot, eigen, far_eigen,
    )
    reduced = sum_over(red, "y")
    span = call(range_body, ((32, 8, 8, 128), BF), reduced, basis_in, far_in)
    span = sum_over(span, COL)
    mapped, keep, give = call(
        mapped_body,
        [((8, 12, 8, 128), BF), ((72, 1792), BF), ((72, 1792), BF)],
        span, basis_in, far_in,
    )
    mapped = swap(call(gram_sum_body, ((8, 12, 8, 128), BF), swap(mapped, "y")), "y")
    core = call(core_body, ((768, 128), BF), mapped, scaled)
    core = swap(core.reshape(32, 3, 8, 128), COL)
    inverse = call(inverse_body, ((72, 128), F32), mapped)
    core, inverse, give = lax.optimization_barrier((core, inverse, give))
    core = call(sum_flat_body, ((768, 128), BF), core)
    core = swap(core.reshape(32, 3, 8, 128), COL)
    both_inverses = lax.all_gather(inverse, "core")
    core, both_inverses, got = lax.optimization_barrier((core, both_inverses, from_sibling(give)))
    part = call(project_body, ((576, 256), BF), core, basis_out, far_out)
    basis = call(basis_body, ((2, 72, 1792), F32), both_inverses, keep, got)
    mine = call(final_body, ((72, 256), F32), inverse, swap(part.reshape(8, 72, 256), "y"))
    return basis, lax.all_gather(mine, "core")


def solution(mesh):
    split = Mesh(mesh.devices.reshape(8, 2, 8, 4), ("y", "core", "z", "x"))
    return jax.shard_map(
        on_device,
        mesh=split,
        in_specs=(
            P(COL, None, ROW),
            P(ROW, None, COL),
            P(ROW, COL),
            P(COL, ROW),
            P(COL, ROW),
            P(None, COL),
        ),
        out_specs=(P(None, None, ROW), P(None, None, COL)),
        check_vma=False,
    )
```

```python
import jax
import jax.numpy as jnp
from jax import lax
from jax.experimental import pallas as pl
from jax.experimental.pallas import tpu as pltpu
from jax.sharding import Mesh
from jax.sharding import PartitionSpec as P

COL = ("z", "x")
ROW = ("y", "core")
BF = jnp.bfloat16
F32 = jnp.float32
MIB = 1024 * 1024


def call(body, out, *args, limit=52):
    many = isinstance(out, list)
    shapes = [jax.ShapeDtypeStruct(s, d) for s, d in (out if many else [out])]
    got = pl.pallas_call(
        body,
        out_shape=shapes,
        in_specs=[pl.BlockSpec(memory_space=pltpu.VMEM)] * len(args),
        out_specs=[pl.BlockSpec(memory_space=pltpu.VMEM)] * len(shapes),
        compiler_params=pltpu.CompilerParams(vmem_limit_bytes=limit * MIB),
    )(*args)
    return got if many else got[0]


def swap(x, axes):
    return lax.all_to_all(x, axes, 0, 0, tiled=True)


def from_sibling(x):
    return lax.ppermute(x, "core", [(0, 1), (1, 0)])


def dot(a, b, ca=1, cb=0, **kw):
    return lax.dot_general(a, b, (((ca,), (cb,)), ((), ())), preferred_element_type=F32, **kw)


def to_tiles(y, out_ref, slots=None):
    slots = slots or out_ref.shape[1]
    lanes = y.shape[1] // 128
    count = (y.shape[0] // 8) * lanes
    for t in range(out_ref.shape[0] * slots):
        if t < count:
            r, g = divmod(t, lanes)
            tile = y[r * 8 : r * 8 + 8, g * 128 : g * 128 + 128]
        else:
            tile = jnp.zeros((8, 128), F32)
        out_ref[t // slots, t % slots] = tile.astype(BF)


def to_flat_tiles(y, out_ref):
    lanes = y.shape[1] // 128
    count = (y.shape[0] // 8) * lanes

    def tile(t):
        r, g = divmod(t, lanes)
        return y[r * 8 : r * 8 + 8, g * 128 : g * 128 + 128] if t < count else jnp.zeros((8, 128), F32)

    for t in range(0, out_ref.shape[0] // 8, 2):
        pair = jnp.concatenate([tile(t), tile(t + 1)], axis=0)
        out_ref[t * 8 : t * 8 + 16] = pair.astype(BF)


def from_tiles(ref, lanes, rows=72, slots=None):
    slots = slots or ref.shape[1]
    lines = []
    for r in range(rows // 8):
        at = [divmod(r * lanes + g, slots) for g in range(lanes)]
        lines.append(jnp.concatenate([ref[p, s].astype(F32) for p, s in at], axis=1))
    return jnp.concatenate(lines, axis=0)


def sum_one_body(x_ref, out_ref):
    out_ref[...] = jnp.sum(x_ref[...].astype(F32), axis=0).astype(BF)


def summed(pieces, axes):
    own = swap(pieces, axes)
    return call(sum_one_body, (own.shape[1:], BF), own)


def sum_body(x_ref, out_ref):
    total = jnp.sum(x_ref[...].astype(F32), axis=0).astype(BF)
    out_ref[...] = jnp.broadcast_to(total[None], out_ref.shape)


def sum_flat_body(x_ref, out_ref):
    total = jnp.sum(x_ref[...].astype(F32), axis=0).reshape(-1, 128)
    peers = jnp.broadcast_to(total[None], (x_ref.shape[0], *total.shape))
    out_ref[...] = peers.reshape(out_ref.shape).astype(BF)


def sum_over(pieces, axes):
    own = swap(pieces, axes)
    return swap(call(sum_body, (own.shape, BF), own), axes)


def picked(n, to, x):
    rows = lax.broadcasted_iota(jnp.int32, (n, x.shape[0]), 0)
    return dot(jnp.where(rows == to, 1.0, 0.0).astype(BF), x).astype(BF)


def row_numbers(n):
    return lax.broadcasted_iota(jnp.int32, (1, n), 1)


def pack_body(x_ref, out_ref):
    core = lax.axis_index("core")
    m = row_numbers(32)
    token = (m & 15) >> 1
    parts = []
    for other in range(2):
        block = core if other == 0 else 1 - core
        mine = jnp.logical_and((m >> 4) == block, (m & 1) == core)
        parts.append(picked(8, jnp.where(mine, token, -1), x_ref[...]))
    packed = jnp.concatenate(parts, axis=1).astype(F32)
    peers = jnp.broadcast_to(packed[None], (8, *packed.shape))
    out_ref[...] = peers.reshape(out_ref.shape).astype(BF)


def dense_body(x_ref, out_ref):
    m = row_numbers(64)
    token = m & 7
    y = picked(48, jnp.where(token < 6, (m >> 3) * 6 + token, -1), x_ref[...])
    out_ref[...] = jnp.broadcast_to(y[None], out_ref.shape)


def act_body(x_ref, w_ref, v_ref, out_ref):
    n = w_ref.shape[0]
    y = dot(x_ref[:, :n], w_ref[...]) + dot(x_ref[:, n:], v_ref[...])
    out_ref[...] = y.astype(BF)


def grad_body(g_ref, s_ref, w_ref, v_ref, out_ref):
    m = row_numbers(384)
    token = m >> 1
    peer = jnp.floor((token.astype(F32) + 0.5) * (1.0 / 6.0)).astype(jnp.int32)
    to = (peer & 3) * 48 + (peer >> 2) * 6 + token - peer * 6
    g = picked(192, jnp.where((m & 1) == lax.axis_index("core"), to, -1), g_ref[...])
    s = s_ref[...]
    w, v = w_ref[...], v_ref[...]
    top = jnp.concatenate([dot(g, w), dot(g, v)], axis=1)
    low = jnp.concatenate([dot(s, w), dot(s, v)], axis=1)
    to_flat_tiles(jnp.concatenate([top, low], axis=0), out_ref)


def scaled_body(a_ref, g_ref, e_ref, f_ref, scaled_ref, out_ref):
    core = lax.axis_index("core")
    a = jnp.concatenate([a_ref[y, core].astype(F32) for y in range(8)], axis=0).astype(BF)
    g = from_tiles(g_ref, 8, 264)
    both = dot(a.T, g[:192].astype(BF))
    n = e_ref.shape[1]
    left = (both[:, :n] / e_ref[...].astype(F32)).astype(BF)
    right = (both[:, n:] / f_ref[...].astype(F32)).astype(BF)
    s = jnp.concatenate([left, right], axis=1)
    scaled_ref[...] = s
    to_tiles(dot(g[192:].astype(BF), s, 1, 1), out_ref)


def range_body(r_ref, w_ref, v_ref, out_ref):
    r = from_tiles(r_ref, 7).astype(BF)
    both = [dot(r, w_ref[...], 1, 1), dot(r, v_ref[...], 1, 1)]
    to_tiles(jnp.concatenate(both, axis=1), out_ref)


def split3(x):
    hi = x.astype(BF)
    left = x - hi.astype(F32)
    mid = left.astype(BF)
    return hi, mid, (left - mid.astype(F32)).astype(BF)


def gram_at(g):
    return (g, 9) if g < 8 else (7, 6)


def mapped_body(r_ref, w_ref, v_ref, out_ref, keep_ref, give_ref):
    r = from_tiles(r_ref, 28).astype(BF)
    n = w_ref.shape[0]
    keep_ref[...] = r[:, :n]
    give_ref[...] = r[:, n:]
    to_tiles(dot(r[:, :n], w_ref[...]) + dot(r[:, n:], v_ref[...]), out_ref, 9)
    gram = jnp.concatenate([dot(r, r, 1, 1), jnp.zeros((72, 56), F32)], axis=1)
    for g in range(9):
        p, s = gram_at(g)
        for i, part in enumerate(split3(gram[g * 8 : g * 8 + 8])):
            out_ref[p, s + i] = part


def gram_sum_body(x_ref, out_ref):
    total = jnp.sum(x_ref[...].astype(F32), axis=0)
    last = lax.axis_index("y") == 7
    parts = split3(total[9] + total[10] + total[11])
    spare = split3(total[6] + total[7] + total[8])
    for i in range(12):
        tile = total[i].astype(BF)
        if i >= 9:
            tile = parts[i - 9]
        elif i >= 6:
            tile = jnp.where(last, spare[i - 6].astype(F32), total[i]).astype(BF)
        out_ref[:, i] = jnp.broadcast_to(tile[None], (out_ref.shape[0], 8, 128))


def core_body(m_ref, s_ref, out_ref):
    m = from_tiles(m_ref, 7, slots=9).astype(BF)
    to_flat_tiles(dot(m, s_ref[...]), out_ref)


def inverse_body(m_ref, out_ref):
    tiles = []
    for g in range(9):
        p, s = gram_at(g)
        tiles.append(sum(m_ref[p, s + i].astype(F32) for i in range(3)))
    left = jnp.concatenate(tiles, axis=0)
    rows = lax.broadcasted_iota(jnp.int32, (72, 128), 0)
    lanes = lax.broadcasted_iota(jnp.int32, (72, 128), 1)
    below = lax.broadcasted_iota(jnp.int32, (72, 1), 0)
    right = jnp.where(rows == lanes, 1.0, 0.0)
    for k in range(72):
        pivot = left[k : k + 1]
        f = left[:, k : k + 1] / pivot[:, k : k + 1]
        f = jnp.where(below > k, f, 0.0)
        line = right[k : k + 1]
        left = left - f * pivot
        right = right - f * line
    d = jnp.sum(jnp.where(rows == lanes, left, 0.0), axis=1, keepdims=True)
    out_ref[...] = right / jnp.sqrt(d)


def basis_body(w_ref, keep_ref, got_ref, out_ref):
    core = lax.axis_index("core")
    for q, ref in ((core, keep_ref), (1 - core, got_ref)):
        w = w_ref[q][:, :72]
        out_ref[q] = dot(w, ref[...].astype(F32), precision=lax.Precision.HIGHEST)


def project_body(c_ref, w_ref, v_ref, out_ref):
    c = from_tiles(c_ref, 8).astype(BF)
    n = w_ref.shape[1]
    y = dot(c[:, :n], w_ref[...], 1, 1) + dot(c[:, n:], v_ref[...], 1, 1)
    peers = jnp.broadcast_to(y[None], (8, *y.shape))
    out_ref[...] = peers.reshape(out_ref.shape).astype(BF)


def final_body(w_ref, p_ref, out_ref):
    p = jnp.sum(p_ref[...].astype(F32), axis=0)
    out_ref[...] = dot(w_ref[...][:, :72], p, precision=lax.Precision.HIGHEST)


def on_device(acts, grads, basis_in, basis_out, eigen, sketch):
    lines = jnp.pad(acts.reshape(12, 1792), ((0, 4), (0, 0)))
    lines = lax.all_gather(lines, "core").reshape(32, 1792)
    packed = call(pack_body, ((64, 3584), BF), lines)
    packed, own_grads = lax.optimization_barrier((packed, grads))
    all_grads = lax.all_gather(own_grads.reshape(24, 256), ROW).reshape(384, 256)
    near = swap(packed.reshape(8, 8, 3584), "z").reshape(64, 3584)
    near, all_grads, away = lax.optimization_barrier(
        (near, all_grads, (basis_in, basis_out, eigen))
    )
    dense = call(dense_body, ((4, 48, 3584), BF), near)
    far_in, far_out, far_eigen = [from_sibling(w) for w in away]
    g_part = call(
        grad_body, ((2304, 128), BF), all_grads, sketch, basis_out, far_out
    )
    both = swap(dense, "x").reshape(192, 3584)
    both, g_part, far_in, far_eigen = lax.optimization_barrier((both, g_part, far_in, far_eigen))
    g_pieces = swap(g_part.reshape(32, 9, 8, 128), COL)
    a_part = call(act_body, ((192, 896), BF), both, basis_in, far_in)
    a_part, g_pieces = lax.optimization_barrier((a_part, g_pieces))
    g_own = call(sum_flat_body, ((2304, 128), BF), g_pieces)
    a_own = summed(a_part.reshape(8, 24, 896), "y")
    a_own, g_own = lax.optimization_barrier((a_own, g_own))
    g_rot = swap(g_own.reshape(32, 9, 8, 128), COL)
    a_rot = lax.all_gather(a_own, ROW).reshape(8, 2, 24, 896)
    scaled, red = call(
        scaled_body, [((896, 1024), BF), ((8, 8, 8, 128), BF)],
        a_rot, g_rot, eigen, far_eigen,
    )
    reduced = sum_over(red, "y")
    span = call(range_body, ((32, 8, 8, 128), BF), reduced, basis_in, far_in, limit=24)
    span = sum_over(span, COL)
    mapped, keep, give = call(
        mapped_body,
        [((8, 12, 8, 128), BF), ((72, 1792), BF), ((72, 1792), BF)],
        span, basis_in, far_in, limit=24,
    )
    mapped = swap(call(gram_sum_body, ((8, 12, 8, 128), BF), swap(mapped, "y")), "y")
    core = call(core_body, ((768, 128), BF), mapped, scaled)
    core = swap(core.reshape(32, 3, 8, 128), COL)
    inverse = call(inverse_body, ((72, 128), F32), mapped)
    core, inverse, give = lax.optimization_barrier((core, inverse, give))
    core = call(sum_flat_body, ((768, 128), BF), core)
    core = swap(core.reshape(32, 3, 8, 128), COL)
    both_inverses = lax.all_gather(inverse, "core")
    core, both_inverses, got = lax.optimization_barrier((core, both_inverses, from_sibling(give)))
    part = call(project_body, ((576, 256), BF), core, basis_out, far_out)
    basis = call(basis_body, ((2, 72, 1792), F32), both_inverses, keep, got)
    mine = call(final_body, ((72, 256), F32), inverse, swap(part.reshape(8, 72, 256), "y"))
    return basis, lax.all_gather(mine, "core")


def solution(mesh):
    split = Mesh(mesh.devices.reshape(8, 2, 8, 4), ("y", "core", "z", "x"))
    return jax.shard_map(
        on_device,
        mesh=split,
        in_specs=(
            P(COL, None, ROW),
            P(ROW, None, COL),
            P(ROW, COL),
            P(COL, ROW),
            P(COL, ROW),
            P(None, COL),
        ),
        out_specs=(P(None, None, ROW), P(None, None, COL)),
        check_vma=False,
    )
```

```python
import jax
import jax.numpy as jnp
from jax import lax
from jax.experimental import pallas as pl
from jax.experimental.pallas import tpu as pltpu
from jax.sharding import Mesh
from jax.sharding import PartitionSpec as P

COL = ("z", "x")
ROW = ("y", "core")
BF = jnp.bfloat16
F32 = jnp.float32
MIB = 1024 * 1024


def call(body, out, *args, limit=32):
    many = isinstance(out, list)
    shapes = [jax.ShapeDtypeStruct(s, d) for s, d in (out if many else [out])]
    got = pl.pallas_call(
        body,
        out_shape=shapes,
        in_specs=[pl.BlockSpec(memory_space=pltpu.VMEM)] * len(args),
        out_specs=[pl.BlockSpec(memory_space=pltpu.VMEM)] * len(shapes),
        compiler_params=pltpu.CompilerParams(vmem_limit_bytes=limit * MIB),
    )(*args)
    return got if many else got[0]


def swap(x, axes):
    return lax.all_to_all(x, axes, 0, 0, tiled=True)


def from_sibling(x):
    return lax.ppermute(x, "core", [(0, 1), (1, 0)])


def dot(a, b, ca=1, cb=0, **kw):
    return lax.dot_general(a, b, (((ca,), (cb,)), ((), ())), preferred_element_type=F32, **kw)


def to_tiles(y, out_ref, slots=None):
    slots = slots or out_ref.shape[1]
    lanes = y.shape[1] // 128
    count = (y.shape[0] // 8) * lanes
    for t in range(out_ref.shape[0] * slots):
        if t < count:
            r, g = divmod(t, lanes)
            tile = y[r * 8 : r * 8 + 8, g * 128 : g * 128 + 128]
        else:
            tile = jnp.zeros((8, 128), F32)
        out_ref[t // slots, t % slots] = tile.astype(BF)


def to_flat_tiles(y, out_ref):
    lanes = y.shape[1] // 128
    count = (y.shape[0] // 8) * lanes

    def tile(t):
        r, g = divmod(t, lanes)
        return y[r * 8 : r * 8 + 8, g * 128 : g * 128 + 128] if t < count else jnp.zeros((8, 128), F32)

    for t in range(0, out_ref.shape[0] // 8, 2):
        pair = jnp.concatenate([tile(t), tile(t + 1)], axis=0)
        out_ref[t * 8 : t * 8 + 16] = pair.astype(BF)


def from_tiles(ref, lanes, rows=72, slots=None):
    slots = slots or ref.shape[1]
    lines = []
    for r in range(rows // 8):
        at = [divmod(r * lanes + g, slots) for g in range(lanes)]
        lines.append(jnp.concatenate([ref[p, s].astype(F32) for p, s in at], axis=1))
    return jnp.concatenate(lines, axis=0)


def sum_one_body(x_ref, out_ref):
    out_ref[...] = jnp.sum(x_ref[...].astype(F32), axis=0).astype(BF)


def summed(pieces, axes):
    own = swap(pieces, axes)
    return call(sum_one_body, (own.shape[1:], BF), own)


def sum_body(x_ref, out_ref):
    total = jnp.sum(x_ref[...].astype(F32), axis=0).astype(BF)
    out_ref[...] = jnp.broadcast_to(total[None], out_ref.shape)


def sum_flat_body(x_ref, out_ref):
    total = jnp.sum(x_ref[...].astype(F32), axis=0).reshape(-1, 128)
    peers = jnp.broadcast_to(total[None], (x_ref.shape[0], *total.shape))
    out_ref[...] = peers.reshape(out_ref.shape).astype(BF)


def sum_over(pieces, axes):
    own = swap(pieces, axes)
    return swap(call(sum_body, (own.shape, BF), own), axes)


def picked(n, to, x):
    rows = lax.broadcasted_iota(jnp.int32, (n, x.shape[0]), 0)
    return dot(jnp.where(rows == to, 1.0, 0.0).astype(BF), x).astype(BF)


def row_numbers(n):
    return lax.broadcasted_iota(jnp.int32, (1, n), 1)


def pack_body(x_ref, out_ref):
    core = lax.axis_index("core")
    m = row_numbers(32)
    token = (m & 15) >> 1
    parts = []
    for other in range(2):
        block = core if other == 0 else 1 - core
        mine = jnp.logical_and((m >> 4) == block, (m & 1) == core)
        parts.append(picked(8, jnp.where(mine, token, -1), x_ref[...]))
    packed = jnp.concatenate(parts, axis=1).astype(F32)
    peers = jnp.broadcast_to(packed[None], (8, *packed.shape))
    out_ref[...] = peers.reshape(out_ref.shape).astype(BF)


def dense_body(x_ref, out_ref):
    m = row_numbers(64)
    token = m & 7
    y = picked(48, jnp.where(token < 6, (m >> 3) * 6 + token, -1), x_ref[...])
    out_ref[...] = jnp.broadcast_to(y[None], out_ref.shape)


def act_body(x_ref, w_ref, v_ref, out_ref):
    n = w_ref.shape[0]
    y = dot(x_ref[:, :n], w_ref[...]) + dot(x_ref[:, n:], v_ref[...])
    out_ref[...] = y.astype(BF)


def grad_body(g_ref, s_ref, w_ref, v_ref, out_ref):
    m = row_numbers(384)
    token = m >> 1
    peer = jnp.floor((token.astype(F32) + 0.5) * (1.0 / 6.0)).astype(jnp.int32)
    to = (peer & 3) * 48 + (peer >> 2) * 6 + token - peer * 6
    g = picked(192, jnp.where((m & 1) == lax.axis_index("core"), to, -1), g_ref[...])
    s = s_ref[...]
    w, v = w_ref[...], v_ref[...]
    top = jnp.concatenate([dot(g, w), dot(g, v)], axis=1)
    low = jnp.concatenate([dot(s, w), dot(s, v)], axis=1)
    to_flat_tiles(jnp.concatenate([top, low], axis=0), out_ref)


def scaled_body(a_ref, g_ref, e_ref, f_ref, scaled_ref, out_ref):
    core = lax.axis_index("core")
    a = jnp.concatenate([a_ref[y, core].astype(F32) for y in range(8)], axis=0).astype(BF)
    g = from_tiles(g_ref, 8, 264)
    both = dot(a.T, g[:192].astype(BF))
    n = e_ref.shape[1]
    left = (both[:, :n] / e_ref[...].astype(F32)).astype(BF)
    right = (both[:, n:] / f_ref[...].astype(F32)).astype(BF)
    s = jnp.concatenate([left, right], axis=1)
    scaled_ref[...] = s
    to_tiles(dot(g[192:].astype(BF), s, 1, 1), out_ref)


def range_body(r_ref, w_ref, v_ref, out_ref):
    r = from_tiles(r_ref, 7).astype(BF)
    both = [dot(r, w_ref[...], 1, 1), dot(r, v_ref[...], 1, 1)]
    to_tiles(jnp.concatenate(both, axis=1), out_ref)


def split3(x):
    hi = x.astype(BF)
    left = x - hi.astype(F32)
    mid = left.astype(BF)
    return hi, mid, (left - mid.astype(F32)).astype(BF)


def gram_at(g):
    return (g, 9) if g < 8 else (7, 6)


def mapped_body(r_ref, w_ref, v_ref, out_ref, keep_ref, give_ref):
    r = from_tiles(r_ref, 28).astype(BF)
    n = w_ref.shape[0]
    keep_ref[...] = r[:, :n]
    give_ref[...] = r[:, n:]
    to_tiles(dot(r[:, :n], w_ref[...]) + dot(r[:, n:], v_ref[...]), out_ref, 9)
    gram = jnp.concatenate([dot(r, r, 1, 1), jnp.zeros((72, 56), F32)], axis=1)
    for g in range(9):
        p, s = gram_at(g)
        for i, part in enumerate(split3(gram[g * 8 : g * 8 + 8])):
            out_ref[p, s + i] = part


def gram_sum_body(x_ref, out_ref):
    total = jnp.sum(x_ref[...].astype(F32), axis=0)
    last = lax.axis_index("y") == 7
    parts = split3(total[9] + total[10] + total[11])
    spare = split3(total[6] + total[7] + total[8])
    for i in range(12):
        tile = total[i].astype(BF)
        if i >= 9:
            tile = parts[i - 9]
        elif i >= 6:
            tile = jnp.where(last, spare[i - 6].astype(F32), total[i]).astype(BF)
        out_ref[:, i] = jnp.broadcast_to(tile[None], (out_ref.shape[0], 8, 128))


def core_body(m_ref, s_ref, out_ref):
    m = from_tiles(m_ref, 7, slots=9).astype(BF)
    to_flat_tiles(dot(m, s_ref[...]), out_ref)


def inverse_body(m_ref, out_ref):
    tiles = []
    for g in range(9):
        p, s = gram_at(g)
        tiles.append(sum(m_ref[p, s + i].astype(F32) for i in range(3)))
    left = jnp.concatenate(tiles, axis=0)
    rows = lax.broadcasted_iota(jnp.int32, (72, 128), 0)
    lanes = lax.broadcasted_iota(jnp.int32, (72, 128), 1)
    below = lax.broadcasted_iota(jnp.int32, (72, 1), 0)
    right = jnp.where(rows == lanes, 1.0, 0.0)
    for k in range(72):
        pivot = left[k : k + 1]
        f = left[:, k : k + 1] / pivot[:, k : k + 1]
        f = jnp.where(below > k, f, 0.0)
        line = right[k : k + 1]
        left = left - f * pivot
        right = right - f * line
    d = jnp.sum(jnp.where(rows == lanes, left, 0.0), axis=1, keepdims=True)
    out_ref[...] = right / jnp.sqrt(d)


def basis_body(w_ref, keep_ref, got_ref, out_ref):
    core = lax.axis_index("core")
    for q, ref in ((core, keep_ref), (1 - core, got_ref)):
        w = w_ref[q][:, :72]
        out_ref[q] = dot(w, ref[...].astype(F32), precision=lax.Precision.HIGHEST)


def project_body(c_ref, w_ref, v_ref, out_ref):
    c = from_tiles(c_ref, 8).astype(BF)
    n = w_ref.shape[1]
    y = dot(c[:, :n], w_ref[...], 1, 1) + dot(c[:, n:], v_ref[...], 1, 1)
    peers = jnp.broadcast_to(y[None], (8, *y.shape))
    out_ref[...] = peers.reshape(out_ref.shape).astype(BF)


def final_body(w_ref, p_ref, out_ref):
    p = jnp.sum(p_ref[...].astype(F32), axis=0)
    out_ref[...] = dot(w_ref[...][:, :72], p, precision=lax.Precision.HIGHEST)


def on_device(acts, grads, basis_in, basis_out, eigen, sketch):
    lines = jnp.pad(acts.reshape(12, 1792), ((0, 4), (0, 0)))
    lines = lax.all_gather(lines, "core").reshape(32, 1792)
    packed = call(pack_body, ((64, 3584), BF), lines, limit=62)
    packed, own_grads, away_out = lax.optimization_barrier((packed, grads, basis_out))
    own_grads = own_grads.reshape(24, 256)
    own_grads, away_in = lax.optimization_barrier((own_grads, basis_in))
    far_out = from_sibling(away_out)
    near = swap(packed.reshape(8, 8, 3584), "z").reshape(64, 3584)
    near, own_grads, far_out, away_in = lax.optimization_barrier((near, own_grads, far_out, away_in))
    far_in = from_sibling(away_in)
    dense = call(dense_body, ((4, 48, 3584), BF), near, limit=62)
    all_grads = lax.all_gather(own_grads, ROW).reshape(384, 256)
    g_part = call(
        grad_body, ((2304, 128), BF), all_grads, sketch, basis_out, far_out, limit=62
    )
    both = swap(dense, "x").reshape(192, 3584)
    both, g_part, away, far_in = lax.optimization_barrier((both, g_part, eigen, far_in))
    g_pieces = swap(g_part.reshape(32, 9, 8, 128), COL)
    a_part = call(act_body, ((192, 896), BF), both, basis_in, far_in)
    a_part, g_pieces, far_eigen = lax.optimization_barrier((a_part, g_pieces, from_sibling(away)))
    g_own = call(sum_flat_body, ((2304, 128), BF), g_pieces, limit=62)
    a_own = summed(a_part.reshape(8, 24, 896), "y")
    a_own, g_own = lax.optimization_barrier((a_own, g_own))
    g_rot = swap(g_own.reshape(32, 9, 8, 128), COL)
    a_rot = lax.all_gather(a_own, ROW).reshape(8, 2, 24, 896)
    scaled, red = call(
        scaled_body, [((896, 1024), BF), ((8, 8, 8, 128), BF)],
        a_rot, g_rot, eigen, far_eigen,
    )
    reduced = sum_over(red, "y")
    span = call(range_body, ((32, 8, 8, 128), BF), reduced, basis_in, far_in)
    span = sum_over(span, COL)
    mapped, keep, give = call(
        mapped_body,
        [((8, 12, 8, 128), BF), ((72, 1792), BF), ((72, 1792), BF)],
        span, basis_in, far_in,
    )
    mapped = swap(call(gram_sum_body, ((8, 12, 8, 128), BF), swap(mapped, "y")), "y")
    core = call(core_body, ((768, 128), BF), mapped, scaled)
    core = swap(core.reshape(32, 3, 8, 128), COL)
    inverse = call(inverse_body, ((72, 128), F32), mapped)
    core, inverse, give = lax.optimization_barrier((core, inverse, give))
    core = call(sum_flat_body, ((768, 128), BF), core)
    core = swap(core.reshape(32, 3, 8, 128), COL)
    both_inverses = lax.all_gather(inverse, "core")
    core, both_inverses, got = lax.optimization_barrier((core, both_inverses, from_sibling(give)))
    part = call(project_body, ((576, 256), BF), core, basis_out, far_out)
    basis = call(basis_body, ((2, 72, 1792), F32), both_inverses, keep, got)
    mine = call(final_body, ((72, 256), F32), inverse, swap(part.reshape(8, 72, 256), "y"))
    return basis, lax.all_gather(mine, "core")


def solution(mesh):
    split = Mesh(mesh.devices.reshape(8, 2, 8, 4), ("y", "core", "z", "x"))
    return jax.shard_map(
        on_device,
        mesh=split,
        in_specs=(
            P(COL, None, ROW),
            P(ROW, None, COL),
            P(ROW, COL),
            P(COL, ROW),
            P(COL, ROW),
            P(None, COL),
        ),
        out_specs=(P(None, None, ROW), P(None, None, COL)),
        check_vma=False,
    )
```
